128 devices in a mesh: row: 16 (over z, x_lo, core), col: 8 (over y, x_hi).
Axes of the slice: x: 4 (x_hi: 2, x_lo: 2; x = x_hi * 2 + x_lo), y: 4, z: 4, core: 2. Of those that a mesh axis runs over, the one named last changes fastest.
Arguments:
- cube: bfloat16 [8, 424, 512, 256], P(None, 'col', 'row'), may hold values from -6 to 6
- library_t: bfloat16 [64, 424], replicated, may hold values from -0.3125 to 0.3125
- inverse: float32 [64, 64], replicated, as said below
- weight_h: int32 [512, 2048], P('row', 'col'), may hold values from 0 to 255
- weight_v: int32 [512, 2048], P('row', 'col'), may hold values from 0 to 255
Outputs:
- abundances: float32 [64, 512, 2048], P(None, 'row', 'col')
The draws below stay inside these ranges and needn't reach their ends.
Inputs may be any that keep to these rules, and one draw needn't show every extreme that they name: `inverse`: an order-one matrix of independent entries with a diagonal between 0.6 and 1.4.
All inputs are finite; a program needn't handle non-finite values.
Results may differ from the reference program's by a relative error of at most 0.0003.
Values may be sent and summed in bfloat16 or wider, within the bound.
No kernel may reach another device: no remote copies, remote signals or barrier semaphores. Data moves between devices by JAX's collectives and lax.ppermute only.
A program may use at most 128 MiB of HBM per device.

```python
import jax
import jax.numpy as jnp
from jax import lax

BANDS = 424
ENDMEMBERS = 64
TW = 256
ITERS = 2
STEPS = 2
HEIGHT = 512
WIDTH = 2048
N_COL = 8


def draw_inverse(key, part):
    first, second = jax.random.split(key)
    diag = jax.random.uniform(first, (ENDMEMBERS,), jnp.float32, 0.6, 1.4)
    off = jax.random.normal(second, (ENDMEMBERS, ENDMEMBERS), jnp.float32) * (1.2 / ENDMEMBERS ** 0.5)
    eye = jnp.eye(ENDMEMBERS, dtype=jnp.float32)
    return eye * diag[:, None] + (1.0 - eye) * off


def plant(values, stream_key, least, high):
    index_at = [jax.random.randint(jax.random.fold_in(stream_key, axis), (), 0, length) for axis, length in enumerate(values.shape)]
    widest = values.shape.index(max(values.shape))
    neighbour = index_at[:widest] + [(index_at[widest] + 1) % values.shape[widest]] + index_at[widest + 1:]
    return values.at[tuple(index_at)].set(least).at[tuple(neighbour)].set(high)


def level_of(rng, shape, cuts, low, top_value):
    loudness, own = 1.0, jax.random.fold_in(rng, 6)
    for axis_at, shards_of in cuts:
        draws = jnp.exp(jax.random.uniform(jax.random.fold_in(own, axis_at), (shards_of,), jnp.float32, low / len(cuts), top_value / len(cuts)))
        loudness = loudness * jnp.repeat(draws, shape[axis_at] // shards_of).reshape([-1 if axis == axis_at else 1 for axis in range(len(shape))])
    return loudness


def scatter_about(rng, extent, deviation, bound, cuts=(), held_as=jnp.bfloat16):
    values = jax.random.normal(rng, extent, jnp.float32) * deviation
    if len(cuts) > 0:
        values = level_of(rng, extent, cuts, -0.22, 0.18) * values
    return jnp.clip(values, min=-bound, max=bound).astype(held_as)


def setup_inputs(seed: int = 0) -> dict:
    seeds = jax.random.split(jax.random.key(seed), 6)
    cube = scatter_about(seeds[0], (N_COL, BANDS, HEIGHT, TW), 1.0, 6.0, ((1, 8), (2, 16)))
    library_t = scatter_about(seeds[1], (ENDMEMBERS, BANDS), BANDS ** -0.5, 0.3125)
    inverse = draw_inverse(jax.random.fold_in(seeds[5], 71), 0)
    weight_h = plant(jax.random.randint(seeds[3], (HEIGHT, WIDTH), 0, 256), jax.random.fold_in(seeds[3], 1), 0, 255).astype(jnp.int32)
    weight_v = plant(jax.random.randint(seeds[4], (HEIGHT, WIDTH), 0, 256), jax.random.fold_in(seeds[4], 1), 0, 255).astype(jnp.int32)
    return {"cube": cube, "library_t": library_t, "inverse": inverse, "weight_h": weight_h, "weight_v": weight_v}


KAPPA = 0.24
PENALTY = 0.5
EDGE_SCALE = 1.0 / 255.0


def diffuse(padded, wh_pad, wv_pad):
    center = padded[:, 1:-1, 1:-1]
    right = padded[:, 1:-1, 2:] - center
    left = center - padded[:, 1:-1, :-2]
    down = padded[:, 2:, 1:-1] - center
    upper = center - padded[:, :-2, 1:-1]
    flux = wh_pad[1:-1, 1:-1] * right - wh_pad[1:-1, :-2] * left + wv_pad[1:-1, 1:-1] * down - wv_pad[:-2, 1:-1] * upper
    return center + KAPPA * flux


def reference(cube, library_t, inverse, weight_h, weight_v):
    strips, bands, height, strip_w = cube.shape
    width = strips * strip_w
    count = library_t.shape[0]

    def project_strip(piece):
        return jnp.dot(library_t, piece.reshape(bands, height * strip_w), preferred_element_type=jnp.float32).reshape(count, height, strip_w)

    stacked = lax.map(project_strip, cube)
    projected = jnp.transpose(stacked, (1, 2, 0, 3)).reshape(count, height * width)
    rows = lax.broadcasted_iota(jnp.int32, (height, width), 0)
    cols = lax.broadcasted_iota(jnp.int32, (height, width), 1)
    wh = jnp.where(cols < width - 1, weight_h.astype(jnp.float32) * EDGE_SCALE, jnp.float32(0.0))
    wv = jnp.where(rows < height - 1, weight_v.astype(jnp.float32) * EDGE_SCALE, jnp.float32(0.0))
    wh_pad = jnp.pad(wh, 1)
    wv_pad = jnp.pad(wv, 1)
    kept = jnp.zeros_like(projected)
    dual = jnp.zeros_like(projected)
    result = None
    for it in range(ITERS):
        mixed = jnp.dot(inverse, projected + PENALTY * (kept - dual), precision=lax.Precision.HIGHEST)
        field = (mixed + dual).reshape(count, height, width)
        for step in range(STEPS):
            field = diffuse(jnp.pad(field, ((0, 0), (1, 1), (1, 1))), wh_pad, wv_pad)
        result = jnp.maximum(field, jnp.float32(0.0))
        kept = result.reshape(count, height * width)
        dual = dual + mixed - kept
    return result
```

```python
import functools

import jax
import jax.numpy as jnp
from jax import lax
from jax.experimental import pallas as pl
from jax.experimental.pallas import tpu as pltpu
from jax.sharding import PartitionSpec as P

KAPPA = 0.24
EDGE_SCALE = 1.0 / 255.0
HALO = 4
LANES = 384


def neighbours(axis, low_part, high_part):
    count = lax.axis_size(axis)
    forward = [(i, i + 1) for i in range(count - 1)]
    backward = [(i + 1, i) for i in range(count - 1)]
    return lax.ppermute(high_part, axis, forward), lax.ppermute(low_part, axis, backward)


def ring_lanes(block):
    width = block.shape[-1]
    left, right = neighbours("col", block[..., :HALO], block[..., width - HALO :])
    gap = jnp.zeros(block.shape[:-1] + (LANES - width - 2 * HALO,), block.dtype)
    return jnp.concatenate([right, gap, left], axis=-1)


def split3(x):
    hi = x.astype(jnp.bfloat16)
    lo = (x - hi.astype(jnp.float32)).astype(jnp.bfloat16)
    return jnp.concatenate([hi, hi, lo], axis=0)


def admm_kernel(inv_ref, p_ref, side_ref, top_ref, bottom_ref, wh_ref, wv_ref, out_ref, mixed, z):
    rows, count, width = p_ref.shape
    total = rows + 2 * HALO
    inv = inv_ref[...]

    def mix(x):
        return jnp.dot(inv, split3(x), preferred_element_type=jnp.float32)

    for i in range(HALO):
        mixed[i] = mix(top_ref[i])
        mixed[total - HALO + i] = mix(bottom_ref[i])

    def first(i, _):
        x = jnp.concatenate([p_ref[i], side_ref[i]], axis=1)
        mixed[i + HALO] = mix(x)
        return 0

    lax.fori_loop(0, rows, first, 0, unroll=2)

    def weight(ref, i):
        return jnp.broadcast_to(ref[pl.ds(i, 1), :], (count, LANES))

    def diffuse(src, begin, end, store):
        def body(i, carry):
            here, above = carry
            below = src[i + 1]
            down = weight(wv_ref, i) * (below - here)
            across = weight(wh_ref, i) * (pltpu.roll(here, LANES - 1, 1) - here)
            store(i, here + (across - pltpu.roll(across, 1, 1)) + (down - above))
            return below, down

        here = src[begin]
        above = weight(wv_ref, begin - 1) * (here - src[begin - 1])
        lax.fori_loop(begin, end, body, (here, above))

    def to_z(i, value):
        z[i] = value

    def second(i, smoothed):
        kept = jnp.maximum(smoothed, 0.0)
        before = mixed[i]
        z[i] = mix(kept - 0.5 * before) + (2.0 * before - kept)

    def emit(i, smoothed):
        out_ref[i - HALO] = jnp.maximum(smoothed[:, :width], 0.0)

    diffuse(mixed, 1, total - 1, to_z)
    diffuse(z, 2, total - 2, second)
    diffuse(z, 3, total - 3, to_z)
    diffuse(z, 4, total - 4, emit)


def admm(inv3, projected, side, top, bottom, wh, wv):
    rows, count, width = projected.shape
    total = rows + 2 * HALO
    vmem = pl.BlockSpec(memory_space=pltpu.VMEM)
    out = pl.pallas_call(
        admm_kernel,
        out_shape=jax.ShapeDtypeStruct((rows, count, width), jnp.float32),
        in_specs=[vmem] * 7,
        out_specs=vmem,
        scratch_shapes=[
            pltpu.VMEM((total, count, LANES), jnp.float32),
            pltpu.VMEM((total, count, LANES), jnp.float32),
        ],
        compiler_params=pltpu.CompilerParams(vmem_limit_bytes=40 * 2**20),
    )(inv3, projected, side, top, bottom, wh, wv)
    return jnp.transpose(out, (1, 0, 2))


def per_device(cube, library_t, inverse, weight_h, weight_v):
    col_count = lax.axis_size("col")
    row_count = lax.axis_size("row")
    tile_h, tile_w = weight_h.shape
    rows = lax.axis_index("row") * tile_h + lax.broadcasted_iota(jnp.int32, (tile_h, tile_w), 0)
    cols = lax.axis_index("col") * tile_w + lax.broadcasted_iota(jnp.int32, (tile_h, tile_w), 1)
    wh = jnp.where(cols < tile_w * col_count - 1, weight_h.astype(jnp.float32), 0.0)
    wv = jnp.where(rows < tile_h * row_count - 1, weight_v.astype(jnp.float32), 0.0)
    weights = jnp.stack([wh, wv], axis=1) * (KAPPA * EDGE_SCALE)
    weights = jnp.concatenate([weights, ring_lanes(weights)], axis=-1)
    above, below = neighbours("row", weights[:HALO], weights[tile_h - HALO :])
    weights = jnp.concatenate([above, weights, below], axis=0)

    received = lax.all_to_all(cube, "col", split_axis=0, concat_axis=1, tiled=True)
    projected = jnp.einsum(
        "eb,cbhw->hew", library_t, received, preferred_element_type=jnp.float32
    )
    side = ring_lanes(projected)
    top, bottom = neighbours(
        "row",
        jnp.concatenate([projected[:HALO], side[:HALO]], axis=-1),
        jnp.concatenate([projected[tile_h - HALO :], side[tile_h - HALO :]], axis=-1),
    )
    inv_hi = lax.reduce_precision(inverse, 8, 7)
    inv3 = jnp.concatenate([inv_hi, inverse - inv_hi, inv_hi], axis=1).astype(jnp.bfloat16)
    return admm(inv3, projected, side, top, bottom, weights[:, 0], weights[:, 1])


def solution(mesh):
    return jax.shard_map(
        per_device,
        mesh=mesh,
        in_specs=(P(None, "col", "row", None), P(), P(), P("row", "col"), P("row", "col")),
        out_specs=P(None, "row", "col"),
        check_vma=False,
    )
```

```python
import jax
import jax.numpy as jnp
from jax import lax
from jax.experimental import pallas as pl
from jax.experimental.pallas import tpu as pltpu
from jax.sharding import PartitionSpec as P

KAPPA = 0.24
EDGE_SCALE = 1.0 / 255.0
HALO = 4
LEAD = 16
SPAN = 288
GROUP = 16


def parts3(x, axis):
    hi = x.astype(jnp.bfloat16)
    lo = (x - hi.astype(jnp.float32)).astype(jnp.bfloat16)
    return jnp.concatenate([hi, hi, lo], axis=axis)


def admm_kernel(
    inv_ref, invt_ref, outer_ref, inner_ref, side_ref, top_ref, bottom_ref, wh_ref, wv_ref,
    out_ref, mixed, y, z, turned,
):
    _, count, width = inner_ref.shape
    half = inner_ref.shape[0]
    quarter = half // 2
    deep = half + 2 * HALO
    inv = inv_ref[...]

    def mix_pairs(pairs, slot):
        cat = jnp.concatenate([parts3(x, 0) for pair in pairs for x in pair], axis=1)
        m = jnp.dot(inv, cat, preferred_element_type=jnp.float32)
        for k in range(len(pairs)):
            a = m[:, 2 * k * width : (2 * k + 1) * width]
            b = m[:, (2 * k + 1) * width : (2 * k + 2) * width]
            mixed[slot + k, LEAD : LEAD + width, :] = jnp.transpose(jnp.concatenate([a, b], 0))

    mix_pairs([(top_ref[k], inner_ref[quarter - HALO + k]) for k in range(HALO)], 0)
    mix_pairs([(inner_ref[quarter + k], bottom_ref[k]) for k in range(HALO)], deep - HALO)

    @pl.loop(0, quarter // 2)
    def _(g):
        r = g * 2
        mix_pairs([(outer_ref[r + k], inner_ref[r + k + quarter]) for k in range(2)], r + HALO)
        mix_pairs(
            [(inner_ref[r + k], outer_ref[r + k + quarter]) for k in range(2)],
            r + HALO + quarter,
        )

    side = jnp.dot(inv, parts3(side_ref[...], 0), preferred_element_type=jnp.float32)
    side = jnp.transpose(jnp.concatenate([side[:, :256], side[:, 128:]], axis=0))
    for r in range(deep):
        mixed[r, LEAD - 8 : LEAD, :] = side[8 * r : 8 * r + 8]
        mixed[r, LEAD + width : LEAD + width + 8, :] = side[8 * r : 8 * r + 8]

    def diffuse(src, dst, begin, end):
        @pl.loop(0, (width + 16) // GROUP)
        def _(g):
            c = pl.multiple_of(LEAD - 8 + g * GROUP, 8)
            at, after, before = pl.ds(c, GROUP), pl.ds(c + 1, GROUP), pl.ds(c - 1, GROUP)
            here = src[begin, at]
            above = wv_ref[begin - 1, at] * (here - src[begin - 1, at])
            for i in range(begin, end):
                below = src[i + 1, at]
                down = wv_ref[i, at] * (below - here)
                right = wh_ref[i, at] * (src[i, after] - here)
                left = wh_ref[i, before] * (here - src[i, before])
                dst[i, at] = here + (right - left) + (down - above)
                here, above = below, down

    diffuse(mixed, z, 1, deep - 1)
    diffuse(z, y, 2, deep - 2)
    invt = invt_ref[...]
    used = pl.ds(LEAD - 8, width + 16)

    @pl.loop(2, deep - 2, step=2)
    def _(first):
        for k in range(2):
            kept = jnp.maximum(y[first + k, used], 0.0)
            before = mixed[first + k, used]
            u = parts3(kept - 0.5 * before, 1)
            m = jnp.dot(u, invt, preferred_element_type=jnp.float32)
            z[first + k, used] = m + (2.0 * before - kept)

    diffuse(z, y, 3, deep - 3)
    diffuse(y, z, 4, deep - 4)

    @pl.loop(0, half // 2)
    def _(g):
        for k in range(2):
            r = g * 2 + k
            v = jnp.transpose(jnp.maximum(z[r + HALO, LEAD : LEAD + width], 0.0))
            for h in range(2):
                for t in range(width // 128):
                    turned[t, pl.ds(r + h * half, count, stride=2 * half), :] = v[
                        h * count : (h + 1) * count, t * 128 : (t + 1) * 128
                    ]

    @pl.loop(0, count // 8)
    def _(g):
        for k in range(8):
            e = g * 8 + k
            for t in range(width // 128):
                out_ref[e, :, t * 128 : (t + 1) * 128] = turned[t, pl.ds(e * 2 * half, 2 * half), :]


def admm(inv3, inv3t, outer, inner, side, top, bottom, wh, wv):
    half, count, width = inner.shape
    vmem = pl.BlockSpec(memory_space=pltpu.VMEM)
    field = pltpu.VMEM((half + 2 * HALO, SPAN, 2 * count), jnp.float32)
    return pl.pallas_call(
        admm_kernel,
        out_shape=jax.ShapeDtypeStruct((count, 2 * half, width), jnp.float32),
        in_specs=[vmem] * 9,
        out_specs=vmem,
        scratch_shapes=[
            field,
            field,
            field,
            pltpu.VMEM((width // 128, count * 2 * half, 128), jnp.float32),
        ],
        compiler_params=pltpu.CompilerParams(vmem_limit_bytes=32 * 2**20),
    )(inv3, inv3t, outer, inner, side, top, bottom, wh, wv)


def neighbours(axis, low_part, high_part):
    count = lax.axis_size(axis)
    forward = [(i, i + 1) for i in range(count - 1)]
    backward = [(i + 1, i) for i in range(count - 1)]
    return lax.ppermute(high_part, axis, forward), lax.ppermute(low_part, axis, backward)


def scaled_weights(weight_h, weight_v):
    col_count = lax.axis_size("col")
    row_count = lax.axis_size("row")
    tile_h, tile_w = weight_h.shape
    rows = lax.axis_index("row") * tile_h + lax.broadcasted_iota(jnp.int32, (tile_h, tile_w), 0)
    cols = lax.axis_index("col") * tile_w + lax.broadcasted_iota(jnp.int32, (tile_h, tile_w), 1)
    wh = jnp.where(cols < tile_w * col_count - 1, weight_h.astype(jnp.float32), 0.0)
    wv = jnp.where(rows < tile_h * row_count - 1, weight_v.astype(jnp.float32), 0.0)
    weights = jnp.stack([wh, wv]) * (KAPPA * EDGE_SCALE)
    above, below = neighbours("row", weights[:, :HALO], weights[:, tile_h - HALO :])
    return jnp.concatenate([above, weights, below], axis=1)


def widened(weights):
    left, right = neighbours("col", weights[..., :HALO], weights[..., -HALO:])
    tile_w = weights.shape[2]
    gap = jnp.zeros(weights.shape[:2] + (LEAD - HALO,), jnp.float32)
    tail = jnp.zeros(weights.shape[:2] + (SPAN - LEAD - HALO - tile_w,), jnp.float32)
    return jnp.concatenate([gap, left, weights, right, tail], axis=2)


def held_weights(weights, count, half):
    halves = [weights[:, : half + 2 * HALO, :, None], weights[:, half:, :, None]]
    spread = [jnp.broadcast_to(x, x.shape[:3] + (count,)) for x in halves]
    both = jnp.concatenate(spread, axis=3)
    return both[0], both[1]


def per_device(cube, library_t, inverse, weight_h, weight_v):
    strips, bands, tile_h, tile_w = cube.shape
    count = library_t.shape[0]
    quarter = tile_h // 4
    half = tile_h // 2

    def to_owner(x):
        return lax.all_to_all(x, "col", split_axis=0, concat_axis=0, tiled=True)

    def project(x):
        x = x.reshape(strips * bands, half, tile_w)
        return jnp.einsum("eb,bhw->hew", library_t, x, preferred_element_type=jnp.float32)

    outer = jnp.concatenate([cube[:, :, :quarter], cube[:, :, 3 * quarter :]], axis=2)
    weights = scaled_weights(weight_h, weight_v)
    outer, weights = lax.optimization_barrier((outer, weights))
    outer = to_owner(outer)
    edge = ((0, 0), (0, 0), (0, 0))
    from_right = jnp.pad(cube[1:, :, :, :HALO], ((0, 1),) + edge)
    from_left = jnp.pad(cube[:-1, :, :, tile_w - HALO :], ((1, 0),) + edge)
    border = jnp.concatenate([from_right, from_left], axis=3).reshape(strips, bands, tile_w)
    border = jnp.pad(border, ((0, 0), (0, -bands % 8), (0, 0)))
    inner = cube[:, :, quarter : 3 * quarter].reshape(strips, bands * half, tile_w)
    inner = jnp.concatenate([inner, border], axis=1)
    weights = widened(weights)
    inner, outer, weights = lax.optimization_barrier((inner, outer, weights))
    inner = to_owner(inner)

    wh, wv = held_weights(weights, count, half)
    outer = project(outer)
    top, bottom = neighbours("row", outer[:HALO], outer[half - HALO :])
    border = inner[:, bands * half : bands * half + bands].reshape(strips * bands, tile_w)
    side = jnp.dot(library_t, border, preferred_element_type=jnp.float32)
    ahead = 2 * HALO * HALO
    side_top, side_bottom = neighbours("row", side[:, :ahead], side[:, side.shape[1] - ahead :])
    side = jnp.concatenate([side_top, side, side_bottom, jnp.zeros_like(side[:, : 2 * ahead])], 1)
    inner = project(inner[:, : bands * half])

    inv_hi = lax.reduce_precision(inverse, 8, 7)
    inv_lo = inverse - inv_hi
    inv3 = jnp.concatenate([inv_hi, inv_lo, inv_hi], axis=1).astype(jnp.bfloat16)
    twice = [jnp.kron(jnp.eye(2, dtype=jnp.float32), x.T) for x in (inv_hi, inv_lo, inv_hi)]
    inv3t = jnp.concatenate(twice, axis=0).astype(jnp.bfloat16)
    return admm(inv3, inv3t, outer, inner, side, top, bottom, wh, wv)


def solution(mesh):
    return jax.shard_map(
        per_device,
        mesh=mesh,
        in_specs=(P(None, "col", "row", None), P(), P(), P("row", "col"), P("row", "col")),
        out_specs=P(None, "row", "col"),
        check_vma=False,
    )
```

```python
import jax
import jax.numpy as jnp
from jax import lax
from jax.experimental import pallas as pl
from jax.experimental.pallas import tpu as pltpu
from jax.sharding import PartitionSpec as P

KAPPA = 0.24
EDGE_SCALE = 1.0 / 255.0
HALO = 4
LEAD = 16
SPAN = 288
GROUP = 16
LEVELS = 256.0
STEPS_MAX = 32000.0


def parts3(x, axis):
    hi = x.astype(jnp.bfloat16)
    lo = (x - hi.astype(jnp.float32)).astype(jnp.bfloat16)
    return jnp.concatenate([hi, hi, lo], axis=axis)


def code_kernel(which_ref, x_ref, out_ref):
    blocks = out_ref.shape[0]
    _, rows, count, width = x_ref.shape
    slot = lax.broadcasted_iota(jnp.int32, (16, width), 0)
    for s in range(blocks):
        levels = jnp.zeros((16, width), jnp.float32)
        for r in range(rows):
            x = x_ref[which_ref[s], r]
            top = jnp.max(jnp.max(jnp.abs(x), axis=0, keepdims=True), axis=1, keepdims=True)
            level = jnp.ceil(jnp.log2(jnp.maximum(top, 1e-30)) * LEVELS)
            scale = STEPS_MAX * jnp.exp2(level * (-1.0 / LEVELS))
            q = jnp.round(x * scale).astype(jnp.int32).astype(jnp.int16)
            out_ref[s, r * count : (r + 1) * count] = q
            levels = jnp.where(slot == r, level, levels)
        out_ref[s, rows * count :] = levels.astype(jnp.int32).astype(jnp.int16)


def coded(x, which):
    _, rows, count, width = x.shape
    vmem = pl.BlockSpec(memory_space=pltpu.VMEM)
    return pl.pallas_call(
        code_kernel,
        out_shape=jax.ShapeDtypeStruct((which.shape[0], rows * count + 16, width), jnp.int16),
        in_specs=[pl.BlockSpec(memory_space=pltpu.SMEM), vmem],
        out_specs=vmem,
        compiler_params=pltpu.CompilerParams(vmem_limit_bytes=16 * 2**20),
    )(which, x)


def scales(levels):
    levels = levels.astype(jnp.int32).astype(jnp.float32)
    return jnp.exp2(levels * (1.0 / LEVELS)) * (1.0 / STEPS_MAX)


def finish_kernel(which_ref, own_ref, given_ref, out_ref, first_ref, last_ref, scale):
    rows, count, _ = out_ref.shape
    scale[...] = scales(given_ref[0, rows * count :])
    for r in range(rows):
        q = given_ref[0, r * count : (r + 1) * count].astype(jnp.int32).astype(jnp.float32)
        x = own_ref[which_ref[0], r] + q * scale[r : r + 1]
        out_ref[r] = x
        if r < HALO:
            first_ref[r] = x
        if r >= rows - HALO:
            last_ref[r - rows + HALO] = x


def finished(own, given, which):
    _, rows, count, width = own.shape
    vmem = pl.BlockSpec(memory_space=pltpu.VMEM)
    shapes = [(rows, count, width), (HALO, count, width), (HALO, count, width)]
    return pl.pallas_call(
        finish_kernel,
        out_shape=[jax.ShapeDtypeStruct(x, jnp.float32) for x in shapes],
        in_specs=[pl.BlockSpec(memory_space=pltpu.SMEM), vmem, vmem],
        out_specs=[vmem] * 3,
        scratch_shapes=[pltpu.VMEM((16, width), jnp.float32)],
        compiler_params=pltpu.CompilerParams(vmem_limit_bytes=16 * 2**20),
    )(which, own, given)


def mix_kernel(
    inv_ref, outer_ref, upper_ref, lower_ref, top_ref, bottom_ref,
    mixed_ref, low_ref, high_ref, scale,
):
    quarter, count = outer_ref.shape[0] // 2, outer_ref.shape[1]
    parts, _, width = upper_ref.shape
    deep = mixed_ref.shape[0]
    inv = inv_ref[...]
    for which, ref in enumerate((upper_ref, lower_ref)):
        for s in range(parts):
            scale[which, s] = scales(ref[s, quarter * count :])

    def row(which, r):
        ref = (upper_ref, lower_ref)[which]
        at = pl.ds(r * count, count)
        terms = [
            ref[s, at].astype(jnp.int32).astype(jnp.float32) * scale[which, s, pl.ds(r, 1)]
            for s in range(parts)
        ]
        return sum(terms[1:], terms[0])

    def mix_pairs(pairs, slot):
        cat = jnp.concatenate([parts3(x, 0) for pair in pairs for x in pair], axis=1)
        m = jnp.dot(inv, cat, preferred_element_type=jnp.float32)
        for k in range(len(pairs)):
            a = m[:, 2 * k * width : (2 * k + 1) * width]
            b = m[:, (2 * k + 1) * width : (2 * k + 2) * width]
            turned = jnp.transpose(jnp.concatenate([a, b], 0))
            mixed_ref[slot + k] = turned
            low_ref[slot + k] = turned[:8]
            high_ref[slot + k] = turned[width - 8 :]

    mix_pairs([(top_ref[k], row(0, quarter - HALO + k)) for k in range(HALO)], 0)
    mix_pairs([(row(1, k), bottom_ref[k]) for k in range(HALO)], deep - HALO)

    @pl.loop(0, quarter // 2)
    def _(g):
        r = g * 2
        mix_pairs([(outer_ref[r + k], row(1, r + k)) for k in range(2)], r + HALO)
        mix_pairs(
            [(row(0, r + k), outer_ref[r + k + quarter]) for k in range(2)], r + HALO + quarter
        )


def mix(inv3, outer, upper, lower, top, bottom):
    half, count, width = outer.shape
    deep = half + 2 * HALO
    vmem = pl.BlockSpec(memory_space=pltpu.VMEM)
    shapes = [(deep, width, 2 * count), (deep, 8, 2 * count), (deep, 8, 2 * count)]
    return pl.pallas_call(
        mix_kernel,
        out_shape=[jax.ShapeDtypeStruct(x, jnp.float32) for x in shapes],
        in_specs=[vmem] * 6,
        out_specs=[vmem] * 3,
        scratch_shapes=[pltpu.VMEM((2, upper.shape[0], 16, width), jnp.float32)],
        compiler_params=pltpu.CompilerParams(vmem_limit_bytes=16 * 2**20),
    )(inv3, outer, upper, lower, top, bottom)


def admm_kernel(
    invt_ref, mixed_ref, left_ref, right_ref, wh_ref, wv_ref, out_ref, mixed, y, z, turned
):
    deep, width, lanes = mixed_ref.shape
    count = lanes // 2
    half = deep - 2 * HALO

    @pl.loop(0, deep)
    def _(r):
        mixed[r, LEAD : LEAD + width] = mixed_ref[r]
        mixed[r, LEAD - 8 : LEAD] = left_ref[r]
        mixed[r, LEAD + width : LEAD + width + 8] = right_ref[r]

    def diffuse(src, dst, begin, end):
        @pl.loop(0, (width + 16) // GROUP)
        def _(g):
            c = pl.multiple_of(LEAD - 8 + g * GROUP, 8)
            at, after, before = pl.ds(c, GROUP), pl.ds(c + 1, GROUP), pl.ds(c - 1, GROUP)
            here = src[begin, at]
            above = wv_ref[begin - 1, at] * (here - src[begin - 1, at])
            for i in range(begin, end):
                below = src[i + 1, at]
                down = wv_ref[i, at] * (below - here)
                right = wh_ref[i, at] * (src[i, after] - here)
                left = wh_ref[i, before] * (here - src[i, before])
                dst[i, at] = here + (right - left) + (down - above)
                here, above = below, down

    diffuse(mixed, z, 1, deep - 1)
    diffuse(z, y, 2, deep - 2)
    invt = invt_ref[...]
    used = pl.ds(LEAD - 8, width + 16)

    @pl.loop(2, deep - 2, step=2)
    def _(first):
        for k in range(2):
            kept = jnp.maximum(y[first + k, used], 0.0)
            before = mixed[first + k, used]
            u = parts3(kept - 0.5 * before, 1)
            m = jnp.dot(u, invt, preferred_element_type=jnp.float32)
            z[first + k, used] = m + (2.0 * before - kept)

    diffuse(z, y, 3, deep - 3)
    diffuse(y, z, 4, deep - 4)

    @pl.loop(0, half // 2)
    def _(g):
        for k in range(2):
            r = g * 2 + k
            v = jnp.transpose(jnp.maximum(z[r + HALO, LEAD : LEAD + width], 0.0))
            for h in range(2):
                for t in range(width // 128):
                    turned[t, pl.ds(r + h * half, count, stride=2 * half), :] = v[
                        h * count : (h + 1) * count, t * 128 : (t + 1) * 128
                    ]

    @pl.loop(0, count // 8)
    def _(g):
        for k in range(8):
            e = g * 8 + k
            for t in range(width // 128):
                out_ref[e, :, t * 128 : (t + 1) * 128] = turned[t, pl.ds(e * 2 * half, 2 * half), :]


def admm(inv3t, mixed, left, right, wh, wv):
    deep, width, lanes = mixed.shape
    half = deep - 2 * HALO
    vmem = pl.BlockSpec(memory_space=pltpu.VMEM)
    field = pltpu.VMEM((deep, SPAN, lanes), jnp.float32)
    return pl.pallas_call(
        admm_kernel,
        out_shape=jax.ShapeDtypeStruct((lanes // 2, 2 * half, width), jnp.float32),
        in_specs=[vmem] * 6,
        out_specs=vmem,
        scratch_shapes=[
            field,
            field,
            field,
            pltpu.VMEM((width // 128, lanes * half, 128), jnp.float32),
        ],
        compiler_params=pltpu.CompilerParams(vmem_limit_bytes=32 * 2**20),
    )(inv3t, mixed, left, right, wh, wv)


def neighbours(axis, low_part, high_part):
    count = lax.axis_size(axis)
    forward = [(i, i + 1) for i in range(count - 1)]
    backward = [(i + 1, i) for i in range(count - 1)]
    return lax.ppermute(high_part, axis, forward), lax.ppermute(low_part, axis, backward)


def raw_weights(weight_h, weight_v):
    col_count = lax.axis_size("col")
    row_count = lax.axis_size("row")
    tile_h, tile_w = weight_h.shape
    rows = lax.axis_index("row") * tile_h + lax.broadcasted_iota(jnp.int32, (tile_h, tile_w), 0)
    cols = lax.axis_index("col") * tile_w + lax.broadcasted_iota(jnp.int32, (tile_h, tile_w), 1)
    wh = jnp.where(cols < tile_w * col_count - 1, weight_h, 0)
    wv = jnp.where(rows < tile_h * row_count - 1, weight_v, 0)
    weights = jnp.stack([wh, wv]).astype(jnp.float32)
    above, below = neighbours("row", weights[:, :HALO], weights[:, tile_h - HALO :])
    return jnp.concatenate([above, weights, below], axis=1)


def widened(weights):
    left, right = neighbours("col", weights[..., :HALO], weights[..., -HALO:])
    tile_w = weights.shape[2]
    gap = jnp.zeros(weights.shape[:2] + (LEAD - HALO,), jnp.float32)
    tail = jnp.zeros(weights.shape[:2] + (SPAN - LEAD - HALO - tile_w,), jnp.float32)
    return jnp.concatenate([gap, left, weights, right, tail], axis=2)


def held_weights(weights, count, half):
    deep = half + 2 * HALO
    pair = jnp.stack([weights[:, :deep], weights[:, half:]]).astype(jnp.bfloat16)
    lanes = lax.broadcasted_iota(jnp.int32, (2, 2 * count), 1) // count
    spread = (lanes == lax.broadcasted_iota(jnp.int32, (2, 2 * count), 0)).astype(jnp.bfloat16)
    scale = jnp.float32(KAPPA * EDGE_SCALE)
    return [
        scale * jnp.einsum("hrc,hl->rcl", x, spread, preferred_element_type=jnp.float32)
        for x in (pair[:, 0], pair[:, 1])
    ]


def per_device(cube, library_t, inverse, weight_h, weight_v):
    strips, bands, tile_h, tile_w = cube.shape
    count = library_t.shape[0]
    half, quarter = tile_h // 2, tile_h // 4
    ys = strips // 2
    y, x = lax.axis_index("col") // 2, lax.axis_index("col") % 2
    swap = [(c, c ^ 1) for c in range(strips)]
    groups = [list(range(k, strips, 2)) for k in range(2)]

    def over_y(block):
        return lax.all_to_all(
            block, "col", split_axis=0, concat_axis=0, axis_index_groups=groups, tiled=True
        )

    def project(library, block):
        return jnp.einsum("eb,bhw->hew", library, block, preferred_element_type=jnp.float32)

    by_y = cube.reshape(ys, 2, bands, tile_h, tile_w)
    library = library_t.reshape(count, ys, 2, bands)
    library_x = lax.dynamic_index_in_dim(library, x, 2, keepdims=False)
    library_other = lax.dynamic_index_in_dim(library, 1 - x, 2, keepdims=False)
    library_own = lax.dynamic_index_in_dim(library_x, y, 1, keepdims=False)
    library_pair = lax.dynamic_index_in_dim(library_other, y, 1, keepdims=False)
    library_two = jnp.concatenate([library_own, library_pair], axis=1)
    library_four = library_x.reshape(count, ys * bands)

    def strips_of(source, other, begin):
        rows = source[:, :, :, begin : begin + quarter]
        block = jnp.where((x == 0) ^ other, rows[:, 0], rows[:, 1])
        return jnp.transpose(block, (1, 0, 2, 3)).reshape(bands, ys * quarter, tile_w)

    barrier = lax.optimization_barrier
    upper = strips_of(by_y, True, quarter)
    upper, by_y = barrier((upper, by_y))
    outer = jnp.concatenate([by_y[..., :quarter, :], by_y[..., 3 * quarter :, :]], axis=3)
    outer = jnp.transpose(outer, (0, 2, 1, 3, 4)).reshape(ys, bands, 2 * half, tile_w)
    outer, by_y = barrier((outer, by_y))
    lower = strips_of(by_y, True, 2 * quarter)
    own = [strips_of(by_y, False, quarter), strips_of(by_y, False, 2 * quarter)]
    upper = lax.ppermute(upper, "col", swap)
    outer = over_y(outer)
    lower = lax.ppermute(lower, "col", swap)
    weights = raw_weights(weight_h, weight_v)

    def inner_part(own_rows, other_rows):
        both = jnp.concatenate([own_rows, other_rows], axis=0)
        part = project(library_two, both).reshape(ys, quarter, count, tile_w)
        return coded(part, jnp.arange(ys, dtype=jnp.int32))

    upper = inner_part(own[0], upper)
    upper, outer = barrier((upper, outer))
    upper = over_y(upper)
    outer = project(library_four, outer.reshape(ys * bands, 2 * half, tile_w))
    outer = outer.reshape(2, half, count, tile_w)
    given = coded(outer, jnp.reshape(1 - x, (1,)))
    given, lower, weights = barrier((given, lower, weights))
    given = lax.ppermute(given, "col", swap)
    lower = inner_part(own[1], lower)
    lower, weights = barrier((lower, weights))
    lower = over_y(lower)
    weights = widened(weights)
    outer, first, last = finished(outer, given, jnp.reshape(x, (1,)))
    top, bottom = neighbours("row", first, last)

    inv_hi = lax.reduce_precision(inverse, 8, 7)
    inv_lo = inverse - inv_hi
    inv3 = jnp.concatenate([inv_hi, inv_lo, inv_hi], axis=1).astype(jnp.bfloat16)
    twice = [jnp.kron(jnp.eye(2, dtype=jnp.float32), a.T) for a in (inv_hi, inv_lo, inv_hi)]
    inv3t = jnp.concatenate(twice, axis=0).astype(jnp.bfloat16)
    wh, wv = held_weights(weights, count, half)
    mixed, low, high = mix(inv3, outer, upper, lower, top, bottom)
    left, right = neighbours("col", low, high)
    return admm(inv3t, mixed, left, right, wh, wv)


def solution(mesh):
    return jax.shard_map(
        per_device,
        mesh=mesh,
        in_specs=(P(None, "col", "row", None), P(), P(), P("row", "col"), P("row", "col")),
        out_specs=P(None, "row", "col"),
        check_vma=False,
    )
```

```python
import functools

import jax
import jax.numpy as jnp
from jax import lax
from jax.experimental import pallas as pl
from jax.experimental.pallas import tpu as pltpu
from jax.sharding import PartitionSpec as P

KAPPA = 0.24
EDGE_SCALE = 1.0 / 255.0
HALO = 4
LEAD = 16
SPAN = 288
GROUP = 16
LEVELS = 256.0
STEPS_MAX = 32000.0


def parts3(x, axis):
    hi = x.astype(jnp.bfloat16)
    lo = (x - hi.astype(jnp.float32)).astype(jnp.bfloat16)
    return jnp.concatenate([hi, hi, lo], axis=axis)


def code_kernel(which_ref, x_ref, *out_refs):
    _, rows, count, width = x_ref.shape
    slot = lax.broadcasted_iota(jnp.int32, (16, width), 0)
    for s, out_ref in enumerate(out_refs):
        levels = jnp.zeros((16, width), jnp.float32)
        for r in range(rows):
            x = x_ref[which_ref[s], r]
            top = jnp.max(jnp.max(jnp.abs(x), axis=0, keepdims=True), axis=1, keepdims=True)
            level = jnp.ceil(jnp.log2(jnp.maximum(top, 1e-30)) * LEVELS)
            scale = STEPS_MAX * jnp.exp2(level * (-1.0 / LEVELS))
            q = jnp.round(x * scale).astype(jnp.int32).astype(jnp.int16)
            out_ref[r * count : (r + 1) * count] = q
            levels = jnp.where(slot == r, level, levels)
        out_ref[rows * count :] = levels.astype(jnp.int32).astype(jnp.int16)


def coded(x, which):
    _, rows, count, width = x.shape
    vmem = pl.BlockSpec(memory_space=pltpu.VMEM)
    shape = jax.ShapeDtypeStruct((rows * count + 16, width), jnp.int16)
    return pl.pallas_call(
        code_kernel,
        out_shape=[shape] * len(which),
        in_specs=[pl.BlockSpec(memory_space=pltpu.SMEM), vmem],
        out_specs=[vmem] * len(which),
        compiler_params=pltpu.CompilerParams(vmem_limit_bytes=5 * 2**20),
    )(jnp.stack(which), x)


def scales(levels):
    levels = levels.astype(jnp.int32).astype(jnp.float32)
    return jnp.exp2(levels * (1.0 / LEVELS)) * (1.0 / STEPS_MAX)


def decoded_row(ref, scale, r, count):
    q = ref[pl.ds(r * count, count)].astype(jnp.int32).astype(jnp.float32)
    return q * scale[pl.ds(r, 1)]


def finish_kernel(keep_last, which_ref, own_ref, *refs):
    *part_refs, out_ref, edge_ref, scale = refs
    rows, count, _ = out_ref.shape
    for s, ref in enumerate(part_refs):
        scale[s] = scales(ref[rows * count :])
    for r in range(rows):
        x = own_ref[which_ref[0], r]
        for s, ref in enumerate(part_refs):
            x = x + decoded_row(ref, scale.at[s], r, count)
        out_ref[r] = x
        e = r - (rows - HALO) if keep_last else r
        if 0 <= e < HALO:
            edge_ref[e] = x


def finished(own, which, parts, keep_last):
    _, rows, count, width = own.shape
    vmem = pl.BlockSpec(memory_space=pltpu.VMEM)
    shapes = [(rows, count, width), (HALO, count, width)]
    return pl.pallas_call(
        functools.partial(finish_kernel, keep_last),
        out_shape=[jax.ShapeDtypeStruct(x, jnp.float32) for x in shapes],
        in_specs=[pl.BlockSpec(memory_space=pltpu.SMEM)] + [vmem] * (1 + len(parts)),
        out_specs=[vmem] * 2,
        scratch_shapes=[pltpu.VMEM((len(parts), 16, width), jnp.float32)],
        compiler_params=pltpu.CompilerParams(vmem_limit_bytes=6 * 2**20),
    )(jnp.reshape(which, (1,)), own, *parts)


def mix_kernel(
    which_ref, inv_ref, early_ref, late_ref, own_ref, a_ref, b_ref, c_ref, top_ref, bottom_ref,
    mixed_ref, low_ref, high_ref, scale,
):
    half, count, width = early_ref.shape
    quarter = half // 2
    deep = mixed_ref.shape[0]
    inv = inv_ref[...]
    parts = (a_ref, b_ref, c_ref)
    for s, ref in enumerate(parts):
        scale[s] = scales(ref[quarter * count :])

    def third(r):
        x = own_ref[which_ref[0], r]
        for s, ref in enumerate(parts):
            x = x + decoded_row(ref, scale.at[s], r, count)
        return x

    def mix_pairs(pairs, slot):
        cat = jnp.concatenate([parts3(x, 0) for pair in pairs for x in pair], axis=1)
        m = jnp.dot(inv, cat, preferred_element_type=jnp.float32)
        for k in range(len(pairs)):
            a = m[:, 2 * k * width : (2 * k + 1) * width]
            b = m[:, (2 * k + 1) * width : (2 * k + 2) * width]
            turned = jnp.transpose(jnp.concatenate([a, b], 0))
            mixed_ref[slot + k] = turned
            low_ref[slot + k] = turned[:8]
            high_ref[slot + k] = turned[width - 8 :]

    mix_pairs([(top_ref[k], early_ref[half - HALO + k]) for k in range(HALO)], 0)
    mix_pairs([(third(k), bottom_ref[k]) for k in range(HALO)], deep - HALO)

    @pl.loop(0, quarter // 2)
    def _(g):
        r = g * 2
        mix_pairs([(early_ref[r + k], third(r + k)) for k in range(2)], r + HALO)
        mix_pairs(
            [(early_ref[r + k + quarter], late_ref[r + k]) for k in range(2)], r + HALO + quarter
        )


def mix(which, inv3, early, late, own, parts, top, bottom):
    half, count, width = early.shape
    deep = half + 2 * HALO
    vmem = pl.BlockSpec(memory_space=pltpu.VMEM)
    shapes = [(deep, width, 2 * count), (deep, 8, 2 * count), (deep, 8, 2 * count)]
    return pl.pallas_call(
        mix_kernel,
        out_shape=[jax.ShapeDtypeStruct(x, jnp.float32) for x in shapes],
        in_specs=[pl.BlockSpec(memory_space=pltpu.SMEM)] + [vmem] * 9,
        out_specs=[vmem] * 3,
        scratch_shapes=[pltpu.VMEM((3, 16, width), jnp.float32)],
        compiler_params=pltpu.CompilerParams(vmem_limit_bytes=10 * 2**20),
    )(jnp.reshape(which, (1,)), inv3, early, late, own, *parts, top, bottom)


def admm_kernel(
    invt_ref, mixed_ref, left_ref, right_ref, wh_ref, wv_ref, out_ref, mixed, y, z, turned
):
    deep, width, lanes = mixed_ref.shape
    count = lanes // 2
    half = deep - 2 * HALO

    @pl.loop(0, deep)
    def _(r):
        mixed[r, LEAD : LEAD + width] = mixed_ref[r]
        mixed[r, LEAD - 8 : LEAD] = left_ref[r]
        mixed[r, LEAD + width : LEAD + width + 8] = right_ref[r]

    def diffuse(src, dst, begin, end):
        @pl.loop(0, (width + 16) // GROUP)
        def _(g):
            c = pl.multiple_of(LEAD - 8 + g * GROUP, 8)
            at, after, before = pl.ds(c, GROUP), pl.ds(c + 1, GROUP), pl.ds(c - 1, GROUP)
            here = src[begin, at]
            above = wv_ref[begin - 1, at] * (here - src[begin - 1, at])
            for i in range(begin, end):
                below = src[i + 1, at]
                down = wv_ref[i, at] * (below - here)
                right = wh_ref[i, at] * (src[i, after] - here)
                left = wh_ref[i, before] * (here - src[i, before])
                dst[i, at] = here + (right - left) + (down - above)
                here, above = below, down

    diffuse(mixed, z, 1, deep - 1)
    diffuse(z, y, 2, deep - 2)
    invt = invt_ref[...]
    used = pl.ds(LEAD - 8, width + 16)

    @pl.loop(2, deep - 2, step=2)
    def _(first):
        for k in range(2):
            kept = jnp.maximum(y[first + k, used], 0.0)
            before = mixed[first + k, used]
            u = parts3(kept - 0.5 * before, 1)
            m = jnp.dot(u, invt, preferred_element_type=jnp.float32)
            z[first + k, used] = m + (2.0 * before - kept)

    diffuse(z, y, 3, deep - 3)
    diffuse(y, z, 4, deep - 4)

    @pl.loop(0, half // 2)
    def _(g):
        for k in range(2):
            r = g * 2 + k
            v = jnp.transpose(jnp.maximum(z[r + HALO, LEAD : LEAD + width], 0.0))
            for h in range(2):
                for t in range(width // 128):
                    turned[t, pl.ds(r + h * half, count, stride=2 * half), :] = v[
                        h * count : (h + 1) * count, t * 128 : (t + 1) * 128
                    ]

    @pl.loop(0, count // 8)
    def _(g):
        for k in range(8):
            e = g * 8 + k
            for t in range(width // 128):
                out_ref[e, :, t * 128 : (t + 1) * 128] = turned[t, pl.ds(e * 2 * half, 2 * half), :]


def admm(inv3t, mixed, left, right, wh, wv):
    deep, width, lanes = mixed.shape
    half = deep - 2 * HALO
    vmem = pl.BlockSpec(memory_space=pltpu.VMEM)
    field = pltpu.VMEM((deep, SPAN, lanes), jnp.float32)
    return pl.pallas_call(
        admm_kernel,
        out_shape=jax.ShapeDtypeStruct((lanes // 2, 2 * half, width), jnp.float32),
        in_specs=[vmem] * 6,
        out_specs=vmem,
        scratch_shapes=[
            field,
            field,
            field,
            pltpu.VMEM((width // 128, lanes * half, 128), jnp.float32),
        ],
        compiler_params=pltpu.CompilerParams(vmem_limit_bytes=28 * 2**20),
    )(inv3t, mixed, left, right, wh, wv)


def neighbours(axis, low_part, high_part):
    count = lax.axis_size(axis)
    forward = [(i, i + 1) for i in range(count - 1)]
    backward = [(i + 1, i) for i in range(count - 1)]
    return lax.ppermute(high_part, axis, forward), lax.ppermute(low_part, axis, backward)


def raw_weights(weight_h, weight_v):
    col_count = lax.axis_size("col")
    row_count = lax.axis_size("row")
    tile_h, tile_w = weight_h.shape
    rows = lax.axis_index("row") * tile_h + lax.broadcasted_iota(jnp.int32, (tile_h, tile_w), 0)
    cols = lax.axis_index("col") * tile_w + lax.broadcasted_iota(jnp.int32, (tile_h, tile_w), 1)
    wh = jnp.where(cols < tile_w * col_count - 1, weight_h, 0)
    wv = jnp.where(rows < tile_h * row_count - 1, weight_v, 0)
    return jnp.stack([wh, wv]).astype(jnp.bfloat16)


def heightened(weights):
    tile_h = weights.shape[1]
    above, below = neighbours("row", weights[:, :HALO], weights[:, tile_h - HALO :])
    return jnp.concatenate([above, weights, below], axis=1)


def widened(weights):
    left, right = neighbours("col", weights[..., :HALO], weights[..., -HALO:])
    tile_w = weights.shape[2]
    gap = jnp.zeros(weights.shape[:2] + (LEAD - HALO,), weights.dtype)
    tail = jnp.zeros(weights.shape[:2] + (SPAN - LEAD - HALO - tile_w,), weights.dtype)
    return jnp.concatenate([gap, left, weights, right, tail], axis=2)


def held_weights(weights, count, half):
    deep = half + 2 * HALO
    pair = jnp.stack([weights[:, :deep], weights[:, half:]]).astype(jnp.bfloat16)
    lanes = lax.broadcasted_iota(jnp.int32, (2, 2 * count), 1) // count
    spread = (lanes == lax.broadcasted_iota(jnp.int32, (2, 2 * count), 0)).astype(jnp.bfloat16)
    scale = jnp.float32(KAPPA * EDGE_SCALE)
    return [
        scale * jnp.einsum("hrc,hl->rcl", x, spread, preferred_element_type=jnp.float32)
        for x in (pair[:, 0], pair[:, 1])
    ]


def per_device(cube, library_t, inverse, weight_h, weight_v):
    strips, bands, tile_h, tile_w = cube.shape
    count = library_t.shape[0]
    half, quarter = tile_h // 2, tile_h // 4
    ys = strips // 2
    col = lax.axis_index("col").astype(jnp.int32)
    y, x = lax.shift_right_logical(col, 1), lax.bitwise_and(col, 1)
    columns = [[c for c in range(strips) if c % 2 == k] for k in range(2)]
    swap = [(c, c ^ 1) for c in range(strips)]
    turns = [[(c, (c + 2 * k) % strips) for c in range(strips)] for k in range(ys)]
    barrier = lax.optimization_barrier

    def project(library, block, blocks, rows):
        block = block.reshape(-1, blocks * rows, tile_w)
        p = jnp.einsum("eb,bhw->hew", library, block, preferred_element_type=jnp.float32)
        return p.reshape(blocks, rows, count, tile_w)

    def rows_of(source, side, begin):
        rows = source[:, :, :, begin : begin + quarter]
        rows = jnp.where(side == 0, rows[:, 0], rows[:, 1])
        return jnp.transpose(rows, (1, 0, 2, 3)).reshape(bands, half * 2, tile_w)

    library_own = lax.dynamic_slice_in_dim(library_t, col * bands, bands, axis=1)
    library_pair = lax.dynamic_slice_in_dim(library_t, (col ^ 1) * bands, bands, axis=1)
    library_x = jnp.concatenate([library_own, library_pair], axis=1)
    split = [library_t[:, k * bands : (k + 1) * bands] for k in range(strips)]
    library_y = jnp.where(
        x == 0, jnp.concatenate(split[::2], axis=1), jnp.concatenate(split[1::2], axis=1)
    )

    by_y = cube.reshape(ys, 2, bands, tile_h, tile_w)
    early = jnp.transpose(by_y[..., :half, :], (0, 2, 1, 3, 4))
    early = early.reshape(ys, bands, 2 * half, tile_w)
    early, by_y = barrier((early, by_y))
    late = rows_of(by_y, 1 - x, 3 * quarter)
    late, by_y = barrier((late, by_y))
    third = rows_of(by_y, 1 - x, half)
    early = lax.all_to_all(
        early, "col", split_axis=0, concat_axis=0, axis_index_groups=columns, tiled=True
    )
    late = lax.ppermute(late, "col", swap)
    third, by_y, weight_h = barrier((third, by_y, weight_h))
    weights = heightened(raw_weights(weight_h, weight_v))
    late_own, third_own = rows_of(by_y, x, 3 * quarter), rows_of(by_y, x, half)
    order = [lax.bitwise_and(y + k, ys - 1) for k in range(1, ys)]

    def over_y(parts):
        return [lax.ppermute(p, "col", turns[k + 1]) for k, p in enumerate(parts)]

    third, late, weights = barrier((third, late, weights))
    third = lax.ppermute(third, "col", swap)
    late = project(library_x, jnp.concatenate([late_own, late], axis=0), ys, quarter)
    late_coded = coded(late, order)
    weights, _ = barrier((weights, late_coded))
    late_coded = over_y(late_coded)
    weights = widened(weights)
    early = project(library_y, early, 2, half)
    early_coded = coded(early, [1 - x])[0]
    third, late_coded, weights, _ = barrier((third, late_coded, weights, early_coded))
    early_coded = lax.ppermute(early_coded, "col", swap)
    third = project(library_x, jnp.concatenate([third_own, third], axis=0), ys, quarter)
    third_coded = coded(third, order)
    late_coded, _ = barrier((late_coded, third_coded))
    third_coded = over_y(third_coded)
    late, last = finished(late, y, late_coded, True)
    early, first = finished(early, x, [early_coded], False)
    top, bottom = neighbours("row", first, last)

    wh, wv = held_weights(weights, count, half)
    inv_hi = lax.reduce_precision(inverse, 8, 7)
    inv3 = jnp.concatenate([inv_hi, inverse - inv_hi, inv_hi], axis=1).astype(jnp.bfloat16)
    block = lax.broadcasted_iota(jnp.int32, (2 * count, 2 * count), 0) // count
    block = block == lax.broadcasted_iota(jnp.int32, (2 * count, 2 * count), 1) // count
    twice = jnp.where(block, jnp.tile(inverse.T, (2, 2)), 0.0)
    twice_hi = lax.reduce_precision(twice, 8, 7)
    inv3t = jnp.concatenate([twice_hi, twice - twice_hi, twice_hi], axis=0).astype(jnp.bfloat16)
    mixed, low, high = mix(y, inv3, early, late, third, third_coded, top, bottom)
    left, right = neighbours("col", low, high)
    return admm(inv3t, mixed, left, right, wh, wv)


def solution(mesh):
    return jax.shard_map(
        per_device,
        mesh=mesh,
        in_specs=(P(None, "col", "row", None), P(), P(), P("row", "col"), P("row", "col")),
        out_specs=P(None, "row", "col"),
        check_vma=False,
    )
```

```python
import functools

import jax
import jax.numpy as jnp
from jax import lax
from jax.experimental import pallas as pl
from jax.experimental.pallas import tpu as pltpu
from jax.sharding import PartitionSpec as P

KAPPA = 0.24
EDGE_SCALE = 1.0 / 255.0
HALO = 4
LEAD = 16
SPAN = 288
GROUP = 16
LEVELS = 256.0
STEPS_MAX = 32000.0


def parts3(x, axis):
    hi = x.astype(jnp.bfloat16)
    lo = (x - hi.astype(jnp.float32)).astype(jnp.bfloat16)
    return jnp.concatenate([hi, hi, lo], axis=axis)


def code_kernel(which_ref, x_ref, *out_refs):
    _, rows, count, width = x_ref.shape
    slot = lax.broadcasted_iota(jnp.int32, (16, width), 0)
    for s, out_ref in enumerate(out_refs):
        levels = jnp.zeros((16, width), jnp.float32)
        for r in range(rows):
            x = x_ref[which_ref[s], r]
            top = jnp.max(jnp.max(jnp.abs(x), axis=0, keepdims=True), axis=1, keepdims=True)
            level = jnp.ceil(jnp.log2(jnp.maximum(top, 1e-30)) * LEVELS)
            scale = STEPS_MAX * jnp.exp2(level * (-1.0 / LEVELS))
            q = jnp.round(x * scale).astype(jnp.int32).astype(jnp.int16)
            out_ref[r * count : (r + 1) * count] = q
            levels = jnp.where(slot == r, level, levels)
        out_ref[rows * count :] = levels.astype(jnp.int32).astype(jnp.int16)


def coded(x, which):
    _, rows, count, width = x.shape
    vmem = pl.BlockSpec(memory_space=pltpu.VMEM)
    shape = jax.ShapeDtypeStruct((rows * count + 16, width), jnp.int16)
    return pl.pallas_call(
        code_kernel,
        out_shape=[shape] * len(which),
        in_specs=[pl.BlockSpec(memory_space=pltpu.SMEM), vmem],
        out_specs=[vmem] * len(which),
        compiler_params=pltpu.CompilerParams(vmem_limit_bytes=5 * 2**20),
    )(jnp.stack(which), x)


def scales(levels):
    levels = levels.astype(jnp.int32).astype(jnp.float32)
    return jnp.exp2(levels * (1.0 / LEVELS)) * (1.0 / STEPS_MAX)


def decoded_row(ref, scale, r, count):
    q = ref[pl.ds(r * count, count)].astype(jnp.int32).astype(jnp.float32)
    return q * scale[pl.ds(r, 1)]


def finish_kernel(keep_last, which_ref, own_ref, *refs):
    *part_refs, out_ref, edge_ref, scale = refs
    rows, count, _ = out_ref.shape
    for s, ref in enumerate(part_refs):
        scale[s] = scales(ref[rows * count :])
    for r in range(rows):
        x = own_ref[which_ref[0], r]
        for s, ref in enumerate(part_refs):
            x = x + decoded_row(ref, scale.at[s], r, count)
        out_ref[r] = x
        e = r - (rows - HALO) if keep_last else r
        if 0 <= e < HALO:
            edge_ref[e] = x


def finished(own, which, parts, keep_last):
    _, rows, count, width = own.shape
    vmem = pl.BlockSpec(memory_space=pltpu.VMEM)
    shapes = [(rows, count, width), (HALO, count, width)]
    return pl.pallas_call(
        functools.partial(finish_kernel, keep_last),
        out_shape=[jax.ShapeDtypeStruct(x, jnp.float32) for x in shapes],
        in_specs=[pl.BlockSpec(memory_space=pltpu.SMEM)] + [vmem] * (1 + len(parts)),
        out_specs=[vmem] * 2,
        scratch_shapes=[pltpu.VMEM((len(parts), 16, width), jnp.float32)],
        compiler_params=pltpu.CompilerParams(vmem_limit_bytes=6 * 2**20),
    )(jnp.reshape(which, (1,)), own, *parts)


def clear_sides(ref):
    for r in range(ref.shape[0]):
        ref[r, :LEAD] = jnp.zeros((LEAD, ref.shape[2]), jnp.float32)
        ref[r, SPAN - LEAD :] = jnp.zeros((LEAD, ref.shape[2]), jnp.float32)


def mix_kernel(
    which_ref, inv_ref, early_ref, late_ref, own_ref, a_ref, b_ref, c_ref, top_ref, bottom_ref,
    mixed_ref, low_ref, high_ref, scale,
):
    half, count, width = early_ref.shape
    quarter = half // 2
    deep = mixed_ref.shape[0]
    inv = inv_ref[...]
    parts = (a_ref, b_ref, c_ref)
    for s, ref in enumerate(parts):
        scale[s] = scales(ref[quarter * count :])
    clear_sides(mixed_ref)

    def third(r):
        x = own_ref[which_ref[0], r]
        for s, ref in enumerate(parts):
            x = x + decoded_row(ref, scale.at[s], r, count)
        return x

    def mix_pairs(pairs, slot):
        cat = jnp.concatenate([parts3(x, 0) for pair in pairs for x in pair], axis=1)
        m = jnp.dot(inv, cat, preferred_element_type=jnp.float32)
        for k in range(len(pairs)):
            a = m[:, 2 * k * width : (2 * k + 1) * width]
            b = m[:, (2 * k + 1) * width : (2 * k + 2) * width]
            turned = jnp.transpose(jnp.concatenate([a, b], 0))
            mixed_ref[slot + k, LEAD : LEAD + width] = turned
            low_ref[slot + k] = turned[:8]
            high_ref[slot + k] = turned[width - 8 :]

    mix_pairs([(top_ref[k], early_ref[half - HALO + k]) for k in range(HALO)], 0)
    mix_pairs([(third(k), bottom_ref[k]) for k in range(HALO)], deep - HALO)

    @pl.loop(0, quarter // 2)
    def _(g):
        r = g * 2
        mix_pairs([(early_ref[r + k], third(r + k)) for k in range(2)], r + HALO)
        mix_pairs(
            [(early_ref[r + k + quarter], late_ref[r + k]) for k in range(2)], r + HALO + quarter
        )


def mix(which, inv3, early, late, own, parts, top, bottom):
    half, count, width = early.shape
    deep = half + 2 * HALO
    vmem = pl.BlockSpec(memory_space=pltpu.VMEM)
    shapes = [(deep, SPAN, 2 * count), (deep, 8, 2 * count), (deep, 8, 2 * count)]
    return pl.pallas_call(
        mix_kernel,
        out_shape=[jax.ShapeDtypeStruct(x, jnp.float32) for x in shapes],
        in_specs=[pl.BlockSpec(memory_space=pltpu.SMEM)] + [vmem] * 9,
        out_specs=[vmem] * 3,
        scratch_shapes=[pltpu.VMEM((3, 16, width), jnp.float32)],
        compiler_params=pltpu.CompilerParams(vmem_limit_bytes=10 * 2**20),
    )(jnp.reshape(which, (1,)), inv3, early, late, own, *parts, top, bottom)


def diffuse(src, wh_ref, wv_ref, rows, columns, group, store):
    @pl.loop(0, (columns[1] - columns[0]) // group)
    def _(g):
        c = pl.multiple_of(columns[0] + g * group, 8)
        at, after, before = pl.ds(c, group), pl.ds(c + 1, group), pl.ds(c - 1, group)
        here = src[rows[0], at]
        above = wv_ref[rows[0] - 1, at] * (here - src[rows[0] - 1, at])
        for i in range(*rows):
            below = src[i + 1, at]
            down = wv_ref[i, at] * (below - here)
            right = wh_ref[i, at] * (src[i, after] - here)
            left = wh_ref[i, before] * (here - src[i, before])
            store(i, c, here + (right - left) + (down - above))
            here, above = below, down


def iterate(mixed, y, z, wh_ref, wv_ref, invt_ref, columns, group, together, store):
    deep, lanes = mixed.shape[0], mixed.shape[2]
    length = columns[1] - columns[0]
    used = pl.ds(columns[0], length)
    invt = invt_ref[...]

    def to(ref):
        def put(i, c, value):
            ref[i, pl.ds(c, group)] = value

        return put

    def step(src, rows, put):
        diffuse(src, wh_ref, wv_ref, rows, columns, group, put)

    step(mixed, (1, deep - 1), to(z))
    step(z, (2, deep - 2), to(y))

    @pl.loop(2, deep - 2, step=together)
    def _(first):
        rows = pl.ds(first, together)
        kept = jnp.maximum(y[rows, used], 0.0).reshape(together * length, lanes)
        before = mixed[rows, used].reshape(together * length, lanes)
        u = parts3(kept - 0.5 * before, 1)
        m = jnp.dot(u, invt, preferred_element_type=jnp.float32)
        z[rows, used] = (m + (2.0 * before - kept)).reshape(together, length, lanes)

    step(z, (3, deep - 3), to(y))
    step(y, (4, deep - 4), store)


def inside_kernel(invt_ref, mixed_ref, wh_ref, wv_ref, out_ref, y, z):
    _, width, _ = out_ref.shape
    clear_sides(y)
    clear_sides(z)

    def store(i, c, value):
        out_ref[i - HALO, pl.ds(pl.multiple_of(c - LEAD, 8), GROUP)] = value

    columns = (LEAD, LEAD + width)
    iterate(mixed_ref, y, z, wh_ref, wv_ref, invt_ref, columns, GROUP, 2, store)


def inside(inv3t, mixed, wh, wv, width):
    deep, span, lanes = mixed.shape
    vmem = pl.BlockSpec(memory_space=pltpu.VMEM)
    field = pltpu.VMEM((deep, span, lanes), jnp.float32)
    return pl.pallas_call(
        inside_kernel,
        out_shape=jax.ShapeDtypeStruct((deep - 2 * HALO, width, lanes), jnp.float32),
        in_specs=[vmem] * 4,
        out_specs=vmem,
        scratch_shapes=[field, field],
        compiler_params=pltpu.CompilerParams(vmem_limit_bytes=22 * 2**20),
        cost_estimate=pl.CostEstimate(
            flops=3 * 10**9, bytes_accessed=24 * 2**20, transcendentals=0
        ),
    )(inv3t, mixed, wh, wv)


def sides_kernel(
    invt_ref, left_ref, low_ref, high_ref, right_ref, wh_ref, wv_ref, inside_ref,
    out_ref, mixed, y, z, turned,
):
    half, width, lanes = inside_ref.shape
    count = lanes // 2
    deep, span, _ = mixed.shape
    for ref in (mixed, y, z):
        ref[...] = jnp.zeros(ref.shape, jnp.float32)
    for at, ref in zip((8, 16, 32, 40), (left_ref, low_ref, high_ref, right_ref)):
        mixed[:, at : at + 8] = ref[...]

    def store(i, c, value):
        z[i, pl.ds(c, span - 16)] = value

    iterate(
        mixed, y, z, wh_ref, wv_ref, invt_ref, (8, span - 8), span - 16, deep - 4, store
    )
    place = lax.broadcasted_iota(jnp.int32, (8, lanes), 0)

    @pl.loop(0, half // 2)
    def _(g):
        for k in range(2):
            r = g * 2 + k
            first = jnp.where(place < HALO, z[r + HALO, 16:24], inside_ref[r, :8])
            last = jnp.where(place < 8 - HALO, inside_ref[r, width - 8 :], z[r + HALO, 32:40])
            whole = jnp.concatenate([first, inside_ref[r, 8 : width - 8], last], axis=0)
            v = jnp.transpose(jnp.maximum(whole, 0.0))
            for h in range(2):
                for t in range(width // 128):
                    turned[t, pl.ds(r + h * half, count, stride=2 * half), :] = v[
                        h * count : (h + 1) * count, t * 128 : (t + 1) * 128
                    ]

    @pl.loop(0, count // 8)
    def _(g):
        for k in range(8):
            e = g * 8 + k
            for t in range(width // 128):
                out_ref[e, :, t * 128 : (t + 1) * 128] = turned[t, pl.ds(e * 2 * half, 2 * half), :]


def sides(inv3t, left, low, high, right, wh, wv, middle):
    half, width, lanes = middle.shape
    vmem = pl.BlockSpec(memory_space=pltpu.VMEM)
    field = pltpu.VMEM(wh.shape, jnp.float32)
    return pl.pallas_call(
        sides_kernel,
        out_shape=jax.ShapeDtypeStruct((lanes // 2, 2 * half, width), jnp.float32),
        in_specs=[vmem] * 8,
        out_specs=vmem,
        scratch_shapes=[
            field,
            field,
            field,
            pltpu.VMEM((width // 128, lanes * half, 128), jnp.float32),
        ],
        compiler_params=pltpu.CompilerParams(vmem_limit_bytes=14 * 2**20),
    )(inv3t, left, low, high, right, wh, wv, middle)


def neighbours(axis, low_part, high_part):
    count = lax.axis_size(axis)
    forward = [(i, i + 1) for i in range(count - 1)]
    backward = [(i + 1, i) for i in range(count - 1)]
    return lax.ppermute(high_part, axis, forward), lax.ppermute(low_part, axis, backward)


def raw_weights(weight_h, weight_v):
    col_count = lax.axis_size("col")
    row_count = lax.axis_size("row")
    tile_h, tile_w = weight_h.shape
    rows = lax.axis_index("row") * tile_h + lax.broadcasted_iota(jnp.int32, (tile_h, tile_w), 0)
    cols = lax.axis_index("col") * tile_w + lax.broadcasted_iota(jnp.int32, (tile_h, tile_w), 1)
    wh = jnp.where(cols < tile_w * col_count - 1, weight_h, 0)
    wv = jnp.where(rows < tile_h * row_count - 1, weight_v, 0)
    return jnp.stack([wh, wv]).astype(jnp.bfloat16)


def heightened(weights):
    tile_h = weights.shape[1]
    above, below = neighbours("row", weights[:, :HALO], weights[:, tile_h - HALO :])
    return jnp.concatenate([above, weights, below], axis=1)


def inside_weights(weights):
    tile_w = weights.shape[2]
    return jnp.pad(weights, ((0, 0), (0, 0), (LEAD, SPAN - LEAD - tile_w)))


def side_parts(weights):
    low, high = weights[..., :8], weights[..., -8:]
    left, right = neighbours("col", low, high)
    gap = jnp.zeros_like(low)
    return [gap, left, low, gap, high, right, gap]


def last_rows_kernel(which_ref, src_ref, out_ref):
    del which_ref
    out_ref[...] = src_ref[...].reshape(out_ref.shape)


def last_rows(source, which, rows):
    blocks, _, bands, height, width = source.shape
    at = height // rows - 1
    return pl.pallas_call(
        last_rows_kernel,
        grid_spec=pltpu.PrefetchScalarGridSpec(
            num_scalar_prefetch=1,
            grid=(blocks,),
            in_specs=[
                pl.BlockSpec((1, 1, bands, rows, width), lambda s, which: (s, which[0], 0, at, 0))
            ],
            out_specs=pl.BlockSpec((1, bands, rows, width), lambda s, which: (s, 0, 0, 0)),
        ),
        out_shape=jax.ShapeDtypeStruct((blocks, bands, rows, width), source.dtype),
    )(jnp.reshape(which, (1,)), source)


def held_weights(weights, count, half):
    deep = half + 2 * HALO
    pair = jnp.stack([weights[:, :deep], weights[:, half:]]).astype(jnp.bfloat16)
    lanes = lax.broadcasted_iota(jnp.int32, (2, 2 * count), 1) // count
    spread = (lanes == lax.broadcasted_iota(jnp.int32, (2, 2 * count), 0)).astype(jnp.bfloat16)
    scale = jnp.float32(KAPPA * EDGE_SCALE)
    return [
        scale * jnp.einsum("hrc,hl->rcl", x, spread, preferred_element_type=jnp.float32)
        for x in (pair[:, 0], pair[:, 1])
    ]


def per_device(cube, library_t, inverse, weight_h, weight_v):
    strips, bands, tile_h, tile_w = cube.shape
    count = library_t.shape[0]
    half, quarter = tile_h // 2, tile_h // 4
    ys = strips // 2
    col = lax.axis_index("col").astype(jnp.int32)
    y, x = lax.shift_right_logical(col, 1), lax.bitwise_and(col, 1)
    columns = [[c for c in range(strips) if c % 2 == k] for k in range(2)]
    swap = [(c, c ^ 1) for c in range(strips)]
    turns = [[(c, (c + 2 * k) % strips) for c in range(strips)] for k in range(ys)]
    barrier = lax.optimization_barrier

    def project(library, block, blocks, rows):
        block = block.reshape(-1, blocks * rows, tile_w)
        p = jnp.einsum("eb,bhw->hew", library, block, preferred_element_type=jnp.float32)
        return p.reshape(blocks, rows, count, tile_w)

    def rows_of(source, side, begin):
        rows = source[:, :, :, begin : begin + quarter]
        rows = jnp.where(side == 0, rows[:, 0], rows[:, 1])
        return jnp.transpose(rows, (1, 0, 2, 3)).reshape(bands, half * 2, tile_w)

    library_own = lax.dynamic_slice_in_dim(library_t, col * bands, bands, axis=1)
    library_pair = lax.dynamic_slice_in_dim(library_t, (col ^ 1) * bands, bands, axis=1)
    library_x = jnp.concatenate([library_own, library_pair], axis=1)
    split = [library_t[:, k * bands : (k + 1) * bands] for k in range(strips)]
    library_y = jnp.where(
        x == 0, jnp.concatenate(split[::2], axis=1), jnp.concatenate(split[1::2], axis=1)
    )

    by_y = cube.reshape(ys, 2, bands, tile_h, tile_w)
    early = jnp.transpose(by_y[..., :half, :], (0, 2, 1, 3, 4))
    early = early.reshape(ys, bands, 2 * half, tile_w)
    early, by_y = barrier((early, by_y))
    late = rows_of(by_y, 1 - x, 3 * quarter)
    late, by_y = barrier((late, by_y))
    third = rows_of(by_y, 1 - x, half)
    early = lax.all_to_all(
        early, "col", split_axis=0, concat_axis=0, axis_index_groups=columns, tiled=True
    )
    late = lax.ppermute(late, "col", swap)
    third, by_y = barrier((third, by_y))
    own, weight_h, weight_v, _ = barrier((last_rows(by_y, x, half), weight_h, weight_v, third))
    weights = heightened(raw_weights(weight_h, weight_v))
    wh, wv = held_weights(inside_weights(weights), count, half)

    def own_rows(begin):
        rows = jnp.transpose(own[:, :, begin : begin + quarter], (1, 0, 2, 3))
        return rows.reshape(bands, ys * quarter, tile_w)

    third_own, late_own = own_rows(0), own_rows(quarter)
    order = [lax.bitwise_and(y + k, ys - 1) for k in range(1, ys)]

    def over_y(parts):
        return [lax.ppermute(p, "col", turns[k + 1]) for k, p in enumerate(parts)]

    third, late = barrier((third, late))
    third = lax.ppermute(third, "col", swap)
    late = project(library_x, jnp.concatenate([late_own, late], axis=0), ys, quarter)
    late_coded = coded(late, order)
    wh, wv, late_coded = barrier((wh, wv, late_coded))
    late_coded = over_y(late_coded)
    early = project(library_y, early, 2, half)
    early_coded = coded(early, [1 - x])[0]
    third, late_coded, _ = barrier((third, late_coded, early_coded))
    early_coded = lax.ppermute(early_coded, "col", swap)
    third = project(library_x, jnp.concatenate([third_own, third], axis=0), ys, quarter)
    third_coded = coded(third, order)
    late_coded, weights, _ = barrier((late_coded, weights, third_coded))
    weights_side = side_parts(weights)
    third_coded = over_y(third_coded)
    late, last = finished(late, y, late_coded, True)
    early, first = finished(early, x, [early_coded], False)
    top, bottom = neighbours("row", first, last)

    weights_side, _, _ = barrier((weights_side, first, last))
    wh_side, wv_side = held_weights(jnp.concatenate(weights_side, axis=2), count, half)
    inv_hi = lax.reduce_precision(inverse, 8, 7)
    inv3 = jnp.concatenate([inv_hi, inverse - inv_hi, inv_hi], axis=1).astype(jnp.bfloat16)
    block = lax.broadcasted_iota(jnp.int32, (2 * count, 2 * count), 0) // count
    block = block == lax.broadcasted_iota(jnp.int32, (2 * count, 2 * count), 1) // count
    twice = jnp.where(block, jnp.tile(inverse.T, (2, 2)), 0.0)
    twice_hi = lax.reduce_precision(twice, 8, 7)
    inv3t = jnp.concatenate([twice_hi, twice - twice_hi, twice_hi], axis=0).astype(jnp.bfloat16)
    mixed, low, high = mix(y, inv3, early, late, third, third_coded, top, bottom)
    left, right = neighbours("col", low, high)
    middle = inside(inv3t, mixed, wh, wv, tile_w)
    return sides(inv3t, left, low, high, right, wh_side, wv_side, middle)


def solution(mesh):
    return jax.shard_map(
        per_device,
        mesh=mesh,
        in_specs=(P(None, "col", "row", None), P(), P(), P("row", "col"), P("row", "col")),
        out_specs=P(None, "row", "col"),
        check_vma=False,
    )
```

```python
import functools

import jax
import jax.numpy as jnp
from jax import lax
from jax.experimental import pallas as pl
from jax.experimental.pallas import tpu as pltpu
from jax.sharding import PartitionSpec as P

KAPPA = 0.24
EDGE_SCALE = 1.0 / 255.0
HALO = 4
LEAD = 16
SPAN = 288
GROUP = 16
LEVELS = 256.0
STEPS_MAX = 32000.0


def parts3(x, axis):
    hi = x.astype(jnp.bfloat16)
    lo = (x - hi.astype(jnp.float32)).astype(jnp.bfloat16)
    return jnp.concatenate([hi, hi, lo], axis=axis)


def code_kernel(which_ref, x_ref, *out_refs):
    _, rows, count, width = x_ref.shape
    slot = lax.broadcasted_iota(jnp.int32, (16, width), 0)
    for s, out_ref in enumerate(out_refs):
        levels = jnp.zeros((16, width), jnp.float32)
        for r in range(rows):
            x = x_ref[which_ref[s], r]
            top = jnp.max(jnp.max(jnp.abs(x), axis=0, keepdims=True), axis=1, keepdims=True)
            level = jnp.ceil(jnp.log2(jnp.maximum(top, 1e-30)) * LEVELS)
            scale = STEPS_MAX * jnp.exp2(level * (-1.0 / LEVELS))
            q = jnp.round(x * scale).astype(jnp.int32).astype(jnp.int16)
            out_ref[r * count : (r + 1) * count] = q
            levels = jnp.where(slot == r, level, levels)
        out_ref[rows * count :] = levels.astype(jnp.int32).astype(jnp.int16)


def coded(x, which):
    _, rows, count, width = x.shape
    vmem = pl.BlockSpec(memory_space=pltpu.VMEM)
    shape = jax.ShapeDtypeStruct((rows * count + 16, width), jnp.int16)
    return pl.pallas_call(
        code_kernel,
        out_shape=[shape] * len(which),
        in_specs=[pl.BlockSpec(memory_space=pltpu.SMEM), vmem],
        out_specs=[vmem] * len(which),
        compiler_params=pltpu.CompilerParams(vmem_limit_bytes=5 * 2**20),
    )(jnp.stack(which), x)


def scales(levels):
    levels = levels.astype(jnp.int32).astype(jnp.float32)
    return jnp.exp2(levels * (1.0 / LEVELS)) * (1.0 / STEPS_MAX)


def decoded_row(ref, scale, r, count):
    q = ref[pl.ds(r * count, count)].astype(jnp.int32).astype(jnp.float32)
    return q * scale[pl.ds(r, 1)]


def finish_kernel(keep_last, which_ref, own_ref, *refs):
    *part_refs, out_ref, edge_ref, scale = refs
    rows, count, _ = out_ref.shape
    for s, ref in enumerate(part_refs):
        scale[s] = scales(ref[rows * count :])
    for r in range(rows):
        x = own_ref[which_ref[0], r]
        for s, ref in enumerate(part_refs):
            x = x + decoded_row(ref, scale.at[s], r, count)
        out_ref[r] = x
        e = r - (rows - HALO) if keep_last else r
        if 0 <= e < HALO:
            edge_ref[e] = x


def finished(own, which, parts, keep_last):
    _, rows, count, width = own.shape
    vmem = pl.BlockSpec(memory_space=pltpu.VMEM)
    shapes = [(rows, count, width), (HALO, count, width)]
    return pl.pallas_call(
        functools.partial(finish_kernel, keep_last),
        out_shape=[jax.ShapeDtypeStruct(x, jnp.float32) for x in shapes],
        in_specs=[pl.BlockSpec(memory_space=pltpu.SMEM)] + [vmem] * (1 + len(parts)),
        out_specs=[vmem] * 2,
        scratch_shapes=[pltpu.VMEM((len(parts), 16, width), jnp.float32)],
        compiler_params=pltpu.CompilerParams(vmem_limit_bytes=6 * 2**20),
    )(jnp.reshape(which, (1,)), own, *parts)


def clear_sides(ref):
    for r in range(ref.shape[0]):
        ref[r, :LEAD] = jnp.zeros((LEAD, ref.shape[2]), jnp.float32)
        ref[r, SPAN - LEAD :] = jnp.zeros((LEAD, ref.shape[2]), jnp.float32)


def mix_kernel(
    which_ref, inv_ref, early_ref, late_ref, own_ref, a_ref, b_ref, c_ref, top_ref, bottom_ref,
    weight_ref,
    mixed_ref, low_ref, high_ref, scale,
):
    half, count, width = early_ref.shape
    quarter = half // 2
    deep = mixed_ref.shape[0]
    inv = inv_ref[...]
    parts = (a_ref, b_ref, c_ref)
    for s, ref in enumerate(parts):
        scale[s] = scales(ref[quarter * count :])
    clear_sides(mixed_ref)
    low_ref[deep] = weight_ref[:8]
    high_ref[deep] = weight_ref[width - 8 :]

    def third(r):
        x = own_ref[which_ref[0], r]
        for s, ref in enumerate(parts):
            x = x + decoded_row(ref, scale.at[s], r, count)
        return x

    def mix_pairs(pairs, slot):
        cat = jnp.concatenate([parts3(x, 0) for pair in pairs for x in pair], axis=1)
        m = jnp.dot(inv, cat, preferred_element_type=jnp.float32)
        for k in range(len(pairs)):
            a = m[:, 2 * k * width : (2 * k + 1) * width]
            b = m[:, (2 * k + 1) * width : (2 * k + 2) * width]
            turned = jnp.transpose(jnp.concatenate([a, b], 0))
            mixed_ref[slot + k, LEAD : LEAD + width] = turned
            low_ref[slot + k] = turned[:8]
            high_ref[slot + k] = turned[width - 8 :]

    mix_pairs([(top_ref[k], early_ref[half - HALO + k]) for k in range(HALO)], 0)
    mix_pairs([(third(k), bottom_ref[k]) for k in range(HALO)], deep - HALO)

    @pl.loop(0, quarter // 2)
    def _(g):
        r = g * 2
        mix_pairs([(early_ref[r + k], third(r + k)) for k in range(2)], r + HALO)
        mix_pairs(
            [(early_ref[r + k + quarter], late_ref[r + k]) for k in range(2)], r + HALO + quarter
        )


def mix(which, inv3, early, late, own, parts, top, bottom, weights):
    half, count, width = early.shape
    deep = half + 2 * HALO
    vmem = pl.BlockSpec(memory_space=pltpu.VMEM)
    shapes = [(deep, SPAN, 2 * count), (deep + 1, 8, 2 * count), (deep + 1, 8, 2 * count)]
    return pl.pallas_call(
        mix_kernel,
        out_shape=[jax.ShapeDtypeStruct(x, jnp.float32) for x in shapes],
        in_specs=[pl.BlockSpec(memory_space=pltpu.SMEM)] + [vmem] * 10,
        out_specs=[vmem] * 3,
        scratch_shapes=[pltpu.VMEM((3, 16, width), jnp.float32)],
        compiler_params=pltpu.CompilerParams(vmem_limit_bytes=10 * 2**20),
    )(jnp.reshape(which, (1,)), inv3, early, late, own, *parts, top, bottom, weights)


def diffuse(src, wh_ref, wv_ref, rows, columns, group, store):
    @pl.loop(0, (columns[1] - columns[0]) // group)
    def _(g):
        c = pl.multiple_of(columns[0] + g * group, 8)
        at, after, before = pl.ds(c, group), pl.ds(c + 1, group), pl.ds(c - 1, group)
        here = src[rows[0], at]
        above = wv_ref[rows[0] - 1, at] * (here - src[rows[0] - 1, at])
        for i in range(*rows):
            below = src[i + 1, at]
            down = wv_ref[i, at] * (below - here)
            right = wh_ref[i, at] * (src[i, after] - here)
            left = wh_ref[i, before] * (here - src[i, before])
            store(i, c, here + (right - left) + (down - above))
            here, above = below, down


def iterate(mixed, y, z, wh_ref, wv_ref, invt_ref, columns, group, together, store):
    deep, lanes = mixed.shape[0], mixed.shape[2]
    length = columns[1] - columns[0]
    used = pl.ds(columns[0], length)
    invt = invt_ref[...]

    def to(ref):
        def put(i, c, value):
            ref[i, pl.ds(c, group)] = value

        return put

    def step(src, rows, put):
        diffuse(src, wh_ref, wv_ref, rows, columns, group, put)

    step(mixed, (1, deep - 1), to(z))
    step(z, (2, deep - 2), to(y))

    @pl.loop(2, deep - 2, step=together)
    def _(first):
        rows = pl.ds(first, together)
        kept = jnp.maximum(y[rows, used], 0.0).reshape(together * length, lanes)
        before = mixed[rows, used].reshape(together * length, lanes)
        u = parts3(kept - 0.5 * before, 1)
        m = jnp.dot(u, invt, preferred_element_type=jnp.float32)
        z[rows, used] = (m + (2.0 * before - kept)).reshape(together, length, lanes)

    step(z, (3, deep - 3), to(y))
    step(y, (4, deep - 4), store)


def inside_kernel(invt_ref, mixed_ref, wh_ref, wv_ref, out_ref, y, z):
    _, width, _ = out_ref.shape
    clear_sides(y)
    clear_sides(z)

    def store(i, c, value):
        out_ref[i - HALO, pl.ds(pl.multiple_of(c - LEAD, 8), GROUP)] = value

    columns = (LEAD, LEAD + width)
    iterate(mixed_ref, y, z, wh_ref, wv_ref, invt_ref, columns, GROUP, 2, store)


def inside(inv3t, mixed, wh, wv, width):
    deep, span, lanes = mixed.shape
    vmem = pl.BlockSpec(memory_space=pltpu.VMEM)
    field = pltpu.VMEM((deep, span, lanes), jnp.float32)
    return pl.pallas_call(
        inside_kernel,
        out_shape=jax.ShapeDtypeStruct((deep - 2 * HALO, width, lanes), jnp.float32),
        in_specs=[vmem] * 4,
        out_specs=vmem,
        scratch_shapes=[field, field],
        compiler_params=pltpu.CompilerParams(vmem_limit_bytes=22 * 2**20),
        cost_estimate=pl.CostEstimate(
            flops=3 * 10**9, bytes_accessed=24 * 2**20, transcendentals=0
        ),
    )(inv3t, mixed, wh, wv)


def sides_kernel(
    invt_ref, left_ref, low_ref, high_ref, right_ref, inside_ref,
    out_ref, mixed, y, z, wh, wv, turned,
):
    half, width, lanes = inside_ref.shape
    count = lanes // 2
    deep, span, _ = mixed.shape
    for ref in (mixed, y, z, wh, wv):
        ref[...] = jnp.zeros(ref.shape, jnp.float32)
    lower = lax.broadcasted_iota(jnp.int32, (8, lanes), 1) < count
    for at, ref in zip((8, 16, 32, 40), (left_ref, low_ref, high_ref, right_ref)):
        mixed[:, at : at + 8] = ref[:deep]
        packed = ref[deep]
        for r in range(deep):
            for weight, lane in ((wh, r), (wv, r + count)):
                one = jnp.broadcast_to(packed[:, lane : lane + 1], (8, lanes))
                two = jnp.broadcast_to(packed[:, lane + half : lane + half + 1], (8, lanes))
                weight[r, at : at + 8] = jnp.where(lower, one, two)

    def store(i, c, value):
        z[i, pl.ds(c, span - 16)] = value

    iterate(
        mixed, y, z, wh, wv, invt_ref, (8, span - 8), span - 16, deep - 4, store
    )
    place = lax.broadcasted_iota(jnp.int32, (8, lanes), 0)

    @pl.loop(0, half // 2)
    def _(g):
        for k in range(2):
            r = g * 2 + k
            first = jnp.where(place < HALO, z[r + HALO, 16:24], inside_ref[r, :8])
            last = jnp.where(place < 8 - HALO, inside_ref[r, width - 8 :], z[r + HALO, 32:40])
            whole = jnp.concatenate([first, inside_ref[r, 8 : width - 8], last], axis=0)
            v = jnp.transpose(jnp.maximum(whole, 0.0))
            for h in range(2):
                for t in range(width // 128):
                    turned[t, pl.ds(r + h * half, count, stride=2 * half), :] = v[
                        h * count : (h + 1) * count, t * 128 : (t + 1) * 128
                    ]

    @pl.loop(0, count // 8)
    def _(g):
        for k in range(8):
            e = g * 8 + k
            for t in range(width // 128):
                out_ref[e, :, t * 128 : (t + 1) * 128] = turned[t, pl.ds(e * 2 * half, 2 * half), :]


def sides(inv3t, left, low, high, right, middle):
    half, width, lanes = middle.shape
    vmem = pl.BlockSpec(memory_space=pltpu.VMEM)
    field = pltpu.VMEM((half + 2 * HALO, 56, lanes), jnp.float32)
    return pl.pallas_call(
        sides_kernel,
        out_shape=jax.ShapeDtypeStruct((lanes // 2, 2 * half, width), jnp.float32),
        in_specs=[vmem] * 6,
        out_specs=vmem,
        scratch_shapes=[
            field,
            field,
            field,
            field,
            field,
            pltpu.VMEM((width // 128, lanes * half, 128), jnp.float32),
        ],
        compiler_params=pltpu.CompilerParams(vmem_limit_bytes=14 * 2**20),
    )(inv3t, left, low, high, right, middle)


def neighbours(axis, low_part, high_part):
    count = lax.axis_size(axis)
    forward = [(i, i + 1) for i in range(count - 1)]
    backward = [(i + 1, i) for i in range(count - 1)]
    return lax.ppermute(high_part, axis, forward), lax.ppermute(low_part, axis, backward)


def raw_weights(weight_h, weight_v):
    col_count = lax.axis_size("col")
    row_count = lax.axis_size("row")
    tile_h, tile_w = weight_h.shape
    rows = lax.axis_index("row") * tile_h + lax.broadcasted_iota(jnp.int32, (tile_h, tile_w), 0)
    cols = lax.axis_index("col") * tile_w + lax.broadcasted_iota(jnp.int32, (tile_h, tile_w), 1)
    wh = jnp.where(cols < tile_w * col_count - 1, weight_h, 0)
    wv = jnp.where(rows < tile_h * row_count - 1, weight_v, 0)
    return jnp.stack([wh, wv]).astype(jnp.bfloat16)


def heightened(weights):
    tile_h = weights.shape[1]
    above, below = neighbours("row", weights[:, :HALO], weights[:, tile_h - HALO :])
    return jnp.concatenate([above, weights, below], axis=1)


def inside_weights(weights):
    tile_w = weights.shape[2]
    return jnp.pad(weights, ((0, 0), (0, 0), (LEAD, SPAN - LEAD - tile_w)))


def packed_weights(weights, count):
    rows, width = weights.shape[1:]
    packed = jnp.pad(weights.astype(jnp.float32), ((0, 0), (0, count - rows), (0, 0)))
    return jnp.transpose(packed.reshape(2 * count, width)) * jnp.float32(KAPPA * EDGE_SCALE)


def last_rows_kernel(which_ref, src_ref, out_ref):
    del which_ref
    out_ref[...] = src_ref[...].reshape(out_ref.shape)


def last_rows(source, which, rows):
    blocks, _, bands, height, width = source.shape
    at = height // rows - 1
    return pl.pallas_call(
        last_rows_kernel,
        grid_spec=pltpu.PrefetchScalarGridSpec(
            num_scalar_prefetch=1,
            grid=(blocks,),
            in_specs=[
                pl.BlockSpec((1, 1, bands, rows, width), lambda s, which: (s, which[0], 0, at, 0))
            ],
            out_specs=pl.BlockSpec((1, bands, rows, width), lambda s, which: (s, 0, 0, 0)),
        ),
        out_shape=jax.ShapeDtypeStruct((blocks, bands, rows, width), source.dtype),
    )(jnp.reshape(which, (1,)), source)


def held_weights(weights, count, half):
    deep = half + 2 * HALO
    pair = jnp.stack([weights[:, :deep], weights[:, half:]]).astype(jnp.bfloat16)
    lanes = lax.broadcasted_iota(jnp.int32, (2, 2 * count), 1) // count
    spread = (lanes == lax.broadcasted_iota(jnp.int32, (2, 2 * count), 0)).astype(jnp.bfloat16)
    scale = jnp.float32(KAPPA * EDGE_SCALE)
    return [
        scale * jnp.einsum("hrc,hl->rcl", x, spread, preferred_element_type=jnp.float32)
        for x in (pair[:, 0], pair[:, 1])
    ]


def per_device(cube, library_t, inverse, weight_h, weight_v):
    strips, bands, tile_h, tile_w = cube.shape
    count = library_t.shape[0]
    half, quarter = tile_h // 2, tile_h // 4
    ys = strips // 2
    col = lax.axis_index("col").astype(jnp.int32)
    y, x = lax.shift_right_logical(col, 1), lax.bitwise_and(col, 1)
    columns = [[c for c in range(strips) if c % 2 == k] for k in range(2)]
    swap = [(c, c ^ 1) for c in range(strips)]
    turns = [[(c, (c + 2 * k) % strips) for c in range(strips)] for k in range(ys)]
    barrier = lax.optimization_barrier

    def project(library, block, blocks, rows):
        block = block.reshape(-1, blocks * rows, tile_w)
        p = jnp.einsum("eb,bhw->hew", library, block, preferred_element_type=jnp.float32)
        return p.reshape(blocks, rows, count, tile_w)

    def rows_of(source, side, begin):
        rows = source[:, :, :, begin : begin + quarter]
        rows = jnp.where(side == 0, rows[:, 0], rows[:, 1])
        return jnp.transpose(rows, (1, 0, 2, 3)).reshape(bands, half * 2, tile_w)

    library_own = lax.dynamic_slice_in_dim(library_t, col * bands, bands, axis=1)
    library_pair = lax.dynamic_slice_in_dim(library_t, (col ^ 1) * bands, bands, axis=1)
    library_x = jnp.concatenate([library_own, library_pair], axis=1)
    split = [library_t[:, k * bands : (k + 1) * bands] for k in range(strips)]
    library_y = jnp.where(
        x == 0, jnp.concatenate(split[::2], axis=1), jnp.concatenate(split[1::2], axis=1)
    )

    by_y = cube.reshape(ys, 2, bands, tile_h, tile_w)
    early = jnp.transpose(by_y[..., :half, :], (0, 2, 1, 3, 4))
    early = early.reshape(ys, bands, 2 * half, tile_w)
    early, by_y = barrier((early, by_y))
    late = rows_of(by_y, 1 - x, 3 * quarter)
    late, by_y = barrier((late, by_y))
    third = rows_of(by_y, 1 - x, half)
    early = lax.all_to_all(
        early, "col", split_axis=0, concat_axis=0, axis_index_groups=columns, tiled=True
    )
    late = lax.ppermute(late, "col", swap)
    third, by_y = barrier((third, by_y))
    own, weight_h, weight_v, _ = barrier((last_rows(by_y, x, half), weight_h, weight_v, third))
    weights = heightened(raw_weights(weight_h, weight_v))
    wh, wv = held_weights(inside_weights(weights), count, half)

    def own_rows(begin):
        rows = jnp.transpose(own[:, :, begin : begin + quarter], (1, 0, 2, 3))
        return rows.reshape(bands, ys * quarter, tile_w)

    third_own, late_own = own_rows(0), own_rows(quarter)
    order = [lax.bitwise_and(y + k, ys - 1) for k in range(1, ys)]

    def over_y(parts):
        return [lax.ppermute(p, "col", turns[k + 1]) for k, p in enumerate(parts)]

    third, late = barrier((third, late))
    third = lax.ppermute(third, "col", swap)
    late = project(library_x, jnp.concatenate([late_own, late], axis=0), ys, quarter)
    late_coded = coded(late, order)
    wh, wv, late_coded = barrier((wh, wv, late_coded))
    late_coded = over_y(late_coded)
    early = project(library_y, early, 2, half)
    early_coded = coded(early, [1 - x])[0]
    third, late_coded, _ = barrier((third, late_coded, early_coded))
    early_coded = lax.ppermute(early_coded, "col", swap)
    third = project(library_x, jnp.concatenate([third_own, third], axis=0), ys, quarter)
    third_coded = coded(third, order)
    late_coded, _ = barrier((late_coded, third_coded))
    packed = packed_weights(weights, count)
    third_coded = over_y(third_coded)
    late, last = finished(late, y, late_coded, True)
    early, first = finished(early, x, [early_coded], False)
    top, bottom = neighbours("row", first, last)

    inv_hi = lax.reduce_precision(inverse, 8, 7)
    inv3 = jnp.concatenate([inv_hi, inverse - inv_hi, inv_hi], axis=1).astype(jnp.bfloat16)
    block = lax.broadcasted_iota(jnp.int32, (2 * count, 2 * count), 0) // count
    block = block == lax.broadcasted_iota(jnp.int32, (2 * count, 2 * count), 1) // count
    twice = jnp.where(block, jnp.tile(inverse.T, (2, 2)), 0.0)
    twice_hi = lax.reduce_precision(twice, 8, 7)
    inv3t = jnp.concatenate([twice_hi, twice - twice_hi, twice_hi], axis=0).astype(jnp.bfloat16)
    mixed, low, high = mix(y, inv3, early, late, third, third_coded, top, bottom, packed)
    left, right = neighbours("col", low, high)
    middle = inside(inv3t, mixed, wh, wv, tile_w)
    return sides(inv3t, left, low, high, right, middle)


def solution(mesh):
    return jax.shard_map(
        per_device,
        mesh=mesh,
        in_specs=(P(None, "col", "row", None), P(), P(), P("row", "col"), P("row", "col")),
        out_specs=P(None, "row", "col"),
        check_vma=False,
    )
```

```python
import functools

import jax
import jax.numpy as jnp
from jax import lax
from jax.experimental import pallas as pl
from jax.experimental.pallas import tpu as pltpu
from jax.sharding import PartitionSpec as P

KAPPA = 0.24
EDGE_SCALE = 1.0 / 255.0
HALO = 4
LEAD = 16
SPAN = 288
GROUP = 16
LEVELS = 256.0
STEPS_MAX = 32000.0


def parts3(x, axis):
    hi = x.astype(jnp.bfloat16)
    lo = (x - hi.astype(jnp.float32)).astype(jnp.bfloat16)
    return jnp.concatenate([hi, hi, lo], axis=axis)


def code_kernel(which_ref, x_ref, *out_refs):
    _, rows, count, width = x_ref.shape
    slot = lax.broadcasted_iota(jnp.int32, (16, width), 0)
    for s, out_ref in enumerate(out_refs):
        levels = jnp.zeros((16, width), jnp.float32)
        for r in range(rows):
            x = x_ref[which_ref[s], r]
            top = jnp.max(jnp.max(jnp.abs(x), axis=0, keepdims=True), axis=1, keepdims=True)
            level = jnp.ceil(jnp.log2(jnp.maximum(top, 1e-30)) * LEVELS)
            scale = STEPS_MAX * jnp.exp2(level * (-1.0 / LEVELS))
            q = jnp.round(x * scale).astype(jnp.int32).astype(jnp.int16)
            out_ref[r * count : (r + 1) * count] = q
            levels = jnp.where(slot == r, level, levels)
        out_ref[rows * count :] = levels.astype(jnp.int32).astype(jnp.int16)


def coded(x, which):
    _, rows, count, width = x.shape
    vmem = pl.BlockSpec(memory_space=pltpu.VMEM)
    shape = jax.ShapeDtypeStruct((rows * count + 16, width), jnp.int16)
    return pl.pallas_call(
        code_kernel,
        out_shape=[shape] * len(which),
        in_specs=[pl.BlockSpec(memory_space=pltpu.SMEM), vmem],
        out_specs=[vmem] * len(which),
        compiler_params=pltpu.CompilerParams(vmem_limit_bytes=5 * 2**20),
    )(jnp.stack(which), x)


def scales(levels):
    levels = levels.astype(jnp.int32).astype(jnp.float32)
    return jnp.exp2(levels * (1.0 / LEVELS)) * (1.0 / STEPS_MAX)


def decoded_row(ref, scale, r, count):
    q = ref[pl.ds(r * count, count)].astype(jnp.int32).astype(jnp.float32)
    return q * scale[pl.ds(r, 1)]


def finish_kernel(keep_last, which_ref, own_ref, *refs):
    *part_refs, out_ref, edge_ref, scale = refs
    rows, count, _ = out_ref.shape
    for s, ref in enumerate(part_refs):
        scale[s] = scales(ref[rows * count :])
    for r in range(rows):
        x = own_ref[which_ref[0], r]
        for s, ref in enumerate(part_refs):
            x = x + decoded_row(ref, scale.at[s], r, count)
        out_ref[r] = x
        e = r - (rows - HALO) if keep_last else r
        if 0 <= e < HALO:
            edge_ref[e] = x


def finished(own, which, parts, keep_last):
    _, rows, count, width = own.shape
    vmem = pl.BlockSpec(memory_space=pltpu.VMEM)
    shapes = [(rows, count, width), (HALO, count, width)]
    return pl.pallas_call(
        functools.partial(finish_kernel, keep_last),
        out_shape=[jax.ShapeDtypeStruct(x, jnp.float32) for x in shapes],
        in_specs=[pl.BlockSpec(memory_space=pltpu.SMEM)] + [vmem] * (1 + len(parts)),
        out_specs=[vmem] * 2,
        scratch_shapes=[pltpu.VMEM((len(parts), 16, width), jnp.float32)],
        compiler_params=pltpu.CompilerParams(vmem_limit_bytes=6 * 2**20),
    )(jnp.reshape(which, (1,)), own, *parts)


def clear_sides(ref):
    for r in range(ref.shape[0]):
        ref[r, :LEAD] = jnp.zeros((LEAD, ref.shape[2]), jnp.float32)
        ref[r, SPAN - LEAD :] = jnp.zeros((LEAD, ref.shape[2]), jnp.float32)


def mix_kernel(
    which_ref, inv_ref, early_ref, late_ref, own_ref, a_ref, b_ref, c_ref, top_ref, bottom_ref,
    weight_ref,
    mixed_ref, low_ref, high_ref, scale,
):
    half, count, width = early_ref.shape
    quarter = half // 2
    deep = mixed_ref.shape[0]
    inv = inv_ref[...]
    parts = (a_ref, b_ref, c_ref)
    for s, ref in enumerate(parts):
        scale[s] = scales(ref[quarter * count :])
    clear_sides(mixed_ref)
    low_ref[deep] = weight_ref[:8]
    high_ref[deep] = weight_ref[width - 8 :]

    def third(r):
        x = own_ref[which_ref[0], r]
        for s, ref in enumerate(parts):
            x = x + decoded_row(ref, scale.at[s], r, count)
        return x

    def mix_pairs(pairs, slot):
        cat = jnp.concatenate([parts3(x, 0) for pair in pairs for x in pair], axis=1)
        m = jnp.dot(inv, cat, preferred_element_type=jnp.float32)
        for k in range(len(pairs)):
            a = m[:, 2 * k * width : (2 * k + 1) * width]
            b = m[:, (2 * k + 1) * width : (2 * k + 2) * width]
            turned = jnp.transpose(jnp.concatenate([a, b], 0))
            mixed_ref[slot + k, LEAD : LEAD + width] = turned
            low_ref[slot + k] = turned[:8]
            high_ref[slot + k] = turned[width - 8 :]

    mix_pairs([(top_ref[k], early_ref[half - HALO + k]) for k in range(HALO)], 0)
    mix_pairs([(third(k), bottom_ref[k]) for k in range(HALO)], deep - HALO)

    @pl.loop(0, quarter // 2)
    def _(g):
        r = g * 2
        mix_pairs([(early_ref[r + k], third(r + k)) for k in range(2)], r + HALO)
        mix_pairs(
            [(early_ref[r + k + quarter], late_ref[r + k]) for k in range(2)], r + HALO + quarter
        )


def mix(which, inv3, early, late, own, parts, top, bottom, weights):
    half, count, width = early.shape
    deep = half + 2 * HALO
    vmem = pl.BlockSpec(memory_space=pltpu.VMEM)
    shapes = [(deep, SPAN, 2 * count), (deep + 1, 8, 2 * count), (deep + 1, 8, 2 * count)]
    return pl.pallas_call(
        mix_kernel,
        out_shape=[jax.ShapeDtypeStruct(x, jnp.float32) for x in shapes],
        in_specs=[pl.BlockSpec(memory_space=pltpu.SMEM)] + [vmem] * 10,
        out_specs=[vmem] * 3,
        scratch_shapes=[pltpu.VMEM((3, 16, width), jnp.float32)],
        compiler_params=pltpu.CompilerParams(vmem_limit_bytes=10 * 2**20),
    )(jnp.reshape(which, (1,)), inv3, early, late, own, *parts, top, bottom, weights)


def diffuse(src, wh_ref, wv_ref, rows, columns, group, store):
    @pl.loop(0, (columns[1] - columns[0]) // group)
    def _(g):
        c = pl.multiple_of(columns[0] + g * group, 8)
        at, after, before = pl.ds(c, group), pl.ds(c + 1, group), pl.ds(c - 1, group)
        here = src[rows[0], at]
        above = wv_ref[rows[0] - 1, at] * (here - src[rows[0] - 1, at])
        for i in range(*rows):
            below = src[i + 1, at]
            down = wv_ref[i, at] * (below - here)
            right = wh_ref[i, at] * (src[i, after] - here)
            left = wh_ref[i, before] * (here - src[i, before])
            store(i, c, here + (right - left) + (down - above))
            here, above = below, down


def iterate(mixed, y, z, wh_ref, wv_ref, invt_ref, columns, group, together, store):
    deep, lanes = mixed.shape[0], mixed.shape[2]
    length = columns[1] - columns[0]
    used = pl.ds(columns[0], length)
    invt = invt_ref[...]

    def to(ref):
        def put(i, c, value):
            ref[i, pl.ds(c, group)] = value

        return put

    def step(src, rows, put):
        diffuse(src, wh_ref, wv_ref, rows, columns, group, put)

    step(mixed, (1, deep - 1), to(z))
    step(z, (2, deep - 2), to(y))

    @pl.loop(2, deep - 2, step=together)
    def _(first):
        rows = pl.ds(first, together)
        kept = jnp.maximum(y[rows, used], 0.0).reshape(together * length, lanes)
        before = mixed[rows, used].reshape(together * length, lanes)
        u = parts3(kept - 0.5 * before, 1)
        m = jnp.dot(u, invt, preferred_element_type=jnp.float32)
        z[rows, used] = (m + (2.0 * before - kept)).reshape(together, length, lanes)

    step(z, (3, deep - 3), to(y))
    step(y, (4, deep - 4), store)


def inside_kernel(invt_ref, mixed_ref, wh_ref, wv_ref, out_ref, y, z):
    _, width, _ = out_ref.shape
    clear_sides(y)
    clear_sides(z)

    def store(i, c, value):
        out_ref[i - HALO, pl.ds(pl.multiple_of(c - LEAD, 8), GROUP)] = value

    columns = (LEAD, LEAD + width)
    iterate(mixed_ref, y, z, wh_ref, wv_ref, invt_ref, columns, GROUP, 2, store)


def inside(inv3t, mixed, wh, wv, width):
    deep, span, lanes = mixed.shape
    vmem = pl.BlockSpec(memory_space=pltpu.VMEM)
    field = pltpu.VMEM((deep, span, lanes), jnp.float32)
    return pl.pallas_call(
        inside_kernel,
        out_shape=jax.ShapeDtypeStruct((deep - 2 * HALO, width, lanes), jnp.float32),
        in_specs=[vmem] * 4,
        out_specs=vmem,
        scratch_shapes=[field, field],
        compiler_params=pltpu.CompilerParams(vmem_limit_bytes=22 * 2**20),
        cost_estimate=pl.CostEstimate(
            flops=3 * 10**9, bytes_accessed=24 * 2**20, transcendentals=0
        ),
    )(inv3t, mixed, wh, wv)


def sides_kernel(
    invt_ref, left_ref, low_ref, high_ref, right_ref, inside_ref,
    out_ref, mixed, y, z, wh, wv, turned,
):
    half, width, lanes = inside_ref.shape
    count = lanes // 2
    deep, span, _ = mixed.shape
    for ref in (mixed, y, z, wh, wv):
        ref[...] = jnp.zeros(ref.shape, jnp.float32)
    lower = lax.broadcasted_iota(jnp.int32, (8, lanes), 1) < count
    for at, ref in zip((8, 16, 32, 40), (left_ref, low_ref, high_ref, right_ref)):
        mixed[:, at : at + 8] = ref[:deep]
        packed = ref[deep]
        for r in range(deep):
            for weight, lane in ((wh, r), (wv, r + count)):
                one = jnp.broadcast_to(packed[:, lane : lane + 1], (8, lanes))
                two = jnp.broadcast_to(packed[:, lane + half : lane + half + 1], (8, lanes))
                weight[r, at : at + 8] = jnp.where(lower, one, two)

    def store(i, c, value):
        z[i, pl.ds(c, span - 16)] = value

    iterate(
        mixed, y, z, wh, wv, invt_ref, (8, span - 8), span - 16, deep - 4, store
    )
    place = lax.broadcasted_iota(jnp.int32, (8, lanes), 0)

    @pl.loop(0, half // 2)
    def _(g):
        for k in range(2):
            r = g * 2 + k
            first = jnp.where(place < HALO, z[r + HALO, 16:24], inside_ref[r, :8])
            last = jnp.where(place < 8 - HALO, inside_ref[r, width - 8 :], z[r + HALO, 32:40])
            whole = jnp.concatenate([first, inside_ref[r, 8 : width - 8], last], axis=0)
            v = jnp.transpose(jnp.maximum(whole, 0.0))
            for h in range(2):
                for t in range(width // 128):
                    turned[t, pl.ds(r + h * half, count, stride=2 * half), :] = v[
                        h * count : (h + 1) * count, t * 128 : (t + 1) * 128
                    ]

    @pl.loop(0, count // 8)
    def _(g):
        for k in range(8):
            e = g * 8 + k
            for t in range(width // 128):
                out_ref[e, :, t * 128 : (t + 1) * 128] = turned[t, pl.ds(e * 2 * half, 2 * half), :]


def sides(inv3t, left, low, high, right, middle):
    half, width, lanes = middle.shape
    vmem = pl.BlockSpec(memory_space=pltpu.VMEM)
    field = pltpu.VMEM((half + 2 * HALO, 56, lanes), jnp.float32)
    return pl.pallas_call(
        sides_kernel,
        out_shape=jax.ShapeDtypeStruct((lanes // 2, 2 * half, width), jnp.float32),
        in_specs=[vmem] * 6,
        out_specs=vmem,
        scratch_shapes=[
            field,
            field,
            field,
            field,
            field,
            pltpu.VMEM((width // 128, lanes * half, 128), jnp.float32),
        ],
        compiler_params=pltpu.CompilerParams(vmem_limit_bytes=14 * 2**20),
    )(inv3t, left, low, high, right, middle)


def neighbours(axis, low_part, high_part):
    count = lax.axis_size(axis)
    forward = [(i, i + 1) for i in range(count - 1)]
    backward = [(i + 1, i) for i in range(count - 1)]
    return lax.ppermute(high_part, axis, forward), lax.ppermute(low_part, axis, backward)


def raw_weights(weight_h, weight_v):
    col_count = lax.axis_size("col")
    row_count = lax.axis_size("row")
    tile_h, tile_w = weight_h.shape
    rows = lax.axis_index("row") * tile_h + lax.broadcasted_iota(jnp.int32, (tile_h, tile_w), 0)
    cols = lax.axis_index("col") * tile_w + lax.broadcasted_iota(jnp.int32, (tile_h, tile_w), 1)
    wh = jnp.where(cols < tile_w * col_count - 1, weight_h, 0)
    wv = jnp.where(rows < tile_h * row_count - 1, weight_v, 0)
    return jnp.stack([wh, wv]).astype(jnp.bfloat16)


def heightened(weights):
    tile_h = weights.shape[1]
    above, below = neighbours("row", weights[:, :HALO], weights[:, tile_h - HALO :])
    return jnp.concatenate([above, weights, below], axis=1)


def inside_weights(weights):
    tile_w = weights.shape[2]
    return jnp.pad(weights, ((0, 0), (0, 0), (LEAD, SPAN - LEAD - tile_w)))


def packed_weights(weights, count):
    rows, width = weights.shape[1:]
    packed = jnp.pad(weights.astype(jnp.float32), ((0, 0), (0, count - rows), (0, 0)))
    return jnp.transpose(packed.reshape(2 * count, width)) * jnp.float32(KAPPA * EDGE_SCALE)


def last_rows_kernel(which_ref, src_ref, out_ref):
    del which_ref
    out_ref[...] = src_ref[...].reshape(out_ref.shape)


def last_rows(source, which, rows):
    blocks, _, bands, height, width = source.shape
    at = height // rows - 1
    return pl.pallas_call(
        last_rows_kernel,
        grid_spec=pltpu.PrefetchScalarGridSpec(
            num_scalar_prefetch=1,
            grid=(blocks,),
            in_specs=[
                pl.BlockSpec((1, 1, bands, rows, width), lambda s, which: (s, which[0], 0, at, 0))
            ],
            out_specs=pl.BlockSpec((1, bands, rows, width), lambda s, which: (s, 0, 0, 0)),
        ),
        out_shape=jax.ShapeDtypeStruct((blocks, bands, rows, width), source.dtype),
    )(jnp.reshape(which, (1,)), source)


def held_weights(weights, count, half):
    deep = half + 2 * HALO
    pair = jnp.stack([weights[:, :deep], weights[:, half:]]).astype(jnp.bfloat16)
    lanes = lax.broadcasted_iota(jnp.int32, (2, 2 * count), 1) // count
    spread = (lanes == lax.broadcasted_iota(jnp.int32, (2, 2 * count), 0)).astype(jnp.bfloat16)
    scale = jnp.float32(KAPPA * EDGE_SCALE)
    return [
        scale * jnp.einsum("hrc,hl->rcl", x, spread, preferred_element_type=jnp.float32)
        for x in (pair[:, 0], pair[:, 1])
    ]


def per_device(cube, library_t, inverse, weight_h, weight_v):
    strips, bands, tile_h, tile_w = cube.shape
    count = library_t.shape[0]
    half, quarter = tile_h // 2, tile_h // 4
    ys = strips // 2
    col = lax.axis_index("col").astype(jnp.int32)
    y, x = lax.shift_right_logical(col, 1), lax.bitwise_and(col, 1)
    columns = [[c for c in range(strips) if c % 2 == k] for k in range(2)]
    swap = [(c, c ^ 1) for c in range(strips)]
    turns = [[(c, (c + 2 * k) % strips) for c in range(strips)] for k in range(ys)]
    barrier = lax.optimization_barrier

    def project(library, block, blocks, rows):
        block = block.reshape(-1, blocks * rows, tile_w)
        p = jnp.einsum("eb,bhw->hew", library, block, preferred_element_type=jnp.float32)
        return p.reshape(blocks, rows, count, tile_w)

    def rows_of(source, side, begin):
        rows = source[:, :, :, begin : begin + quarter]
        rows = jnp.where(side == 0, rows[:, 0], rows[:, 1])
        return jnp.transpose(rows, (1, 0, 2, 3)).reshape(bands, half * 2, tile_w)

    library_own = lax.dynamic_slice_in_dim(library_t, col * bands, bands, axis=1)
    library_pair = lax.dynamic_slice_in_dim(library_t, (col ^ 1) * bands, bands, axis=1)
    library_x = jnp.concatenate([library_own, library_pair], axis=1)
    split = [library_t[:, k * bands : (k + 1) * bands] for k in range(strips)]
    library_y = jnp.where(
        x == 0, jnp.concatenate(split[::2], axis=1), jnp.concatenate(split[1::2], axis=1)
    )

    by_y = cube.reshape(ys, 2, bands, tile_h, tile_w)
    early = jnp.transpose(by_y[..., :half, :], (0, 2, 1, 3, 4))
    early = early.reshape(ys, bands, 2 * half, tile_w)
    early, by_y = barrier((early, by_y))
    late = rows_of(by_y, 1 - x, 3 * quarter)
    late, by_y = barrier((late, by_y))
    third = rows_of(by_y, 1 - x, half)
    early = lax.all_to_all(
        early, "col", split_axis=0, concat_axis=0, axis_index_groups=columns, tiled=True
    )
    late = lax.ppermute(late, "col", swap)
    third, by_y = barrier((third, by_y))
    own, weight_h, weight_v, _ = barrier((last_rows(by_y, x, half), weight_h, weight_v, third))
    weights = heightened(raw_weights(weight_h, weight_v))
    wh, wv = held_weights(inside_weights(weights), count, half)

    def own_rows(begin):
        rows = jnp.transpose(own[:, :, begin : begin + quarter], (1, 0, 2, 3))
        return rows.reshape(bands, ys * quarter, tile_w)

    third_own, late_own = own_rows(0), own_rows(quarter)
    order = [lax.bitwise_and(y + k, ys - 1) for k in range(1, ys)]

    def over_y(parts):
        return [lax.ppermute(p, "col", turns[k + 1]) for k, p in enumerate(parts)]

    third, late = barrier((third, late))
    third = lax.ppermute(third, "col", swap)
    late = project(library_x, jnp.concatenate([late_own, late], axis=0), ys, quarter)
    late_coded = coded(late, order)
    wh, wv, late_coded = barrier((wh, wv, late_coded))
    late_coded = over_y(late_coded)
    early = project(library_y, early, 2, half)
    early_coded = coded(early, [1 - x])[0]
    third, late_coded, _ = barrier((third, late_coded, early_coded))
    early_coded = lax.ppermute(early_coded, "col", swap)
    third = project(library_x, jnp.concatenate([third_own, third], axis=0), ys, quarter)
    third_coded = coded(third, order)
    late_coded, _ = barrier((late_coded, third_coded))
    packed = packed_weights(weights, count)
    third_coded = over_y(third_coded)
    late, last = finished(late, y, late_coded, True)
    early, first = finished(early, x, [early_coded], False)
    top, bottom = neighbours("row", first, last)

    inv_hi = lax.reduce_precision(inverse, 8, 7)
    inv3 = jnp.concatenate([inv_hi, inverse - inv_hi, inv_hi], axis=1).astype(jnp.bfloat16)
    block = lax.broadcasted_iota(jnp.int32, (2 * count, 2 * count), 0) // count
    block = block == lax.broadcasted_iota(jnp.int32, (2 * count, 2 * count), 1) // count
    twice = jnp.where(block, jnp.tile(inverse.T, (2, 2)), 0.0)
    twice_hi = lax.reduce_precision(twice, 8, 7)
    inv3t = jnp.concatenate([twice_hi, twice - twice_hi, twice_hi], axis=0).astype(jnp.bfloat16)
    mixed, low, high = mix(y, inv3, early, late, third, third_coded, top, bottom, packed)
    left, right = neighbours("col", low, high)
    weights_in, _ = barrier((inside_weights(weights), low))
    wv = held_weights(weights_in, count, half)[1]
    middle = inside(inv3t, mixed, wh, wv, tile_w)
    return sides(inv3t, left, low, high, right, middle)


def solution(mesh):
    return jax.shard_map(
        per_device,
        mesh=mesh,
        in_specs=(P(None, "col", "row", None), P(), P(), P("row", "col"), P("row", "col")),
        out_specs=P(None, "row", "col"),
        check_vma=False,
    )
```

```python
import functools

import jax
import jax.numpy as jnp
from jax import lax
from jax.experimental import pallas as pl
from jax.experimental.pallas import tpu as pltpu
from jax.sharding import PartitionSpec as P

KAPPA = 0.24
EDGE_SCALE = 1.0 / 255.0
HALO = 4
LEAD = 16
SPAN = 288
GROUP = 128
LEVELS = 256.0
STEPS_MAX = 32000.0


def parts3(x, axis):
    hi = x.astype(jnp.bfloat16)
    lo = (x - hi.astype(jnp.float32)).astype(jnp.bfloat16)
    return jnp.concatenate([hi, hi, lo], axis=axis)


def code_kernel(which_ref, x_ref, *out_refs):
    _, rows, count, width = x_ref.shape
    slot = lax.broadcasted_iota(jnp.int32, (16, width), 0)
    for s, out_ref in enumerate(out_refs):
        levels = jnp.zeros((16, width), jnp.float32)
        for r in range(rows):
            x = x_ref[which_ref[s], r]
            top = jnp.max(jnp.max(jnp.abs(x), axis=0, keepdims=True), axis=1, keepdims=True)
            level = jnp.ceil(jnp.log2(jnp.maximum(top, 1e-30)) * LEVELS)
            scale = STEPS_MAX * jnp.exp2(level * (-1.0 / LEVELS))
            q = jnp.round(x * scale).astype(jnp.int32).astype(jnp.int16)
            out_ref[r * count : (r + 1) * count] = q
            levels = jnp.where(slot == r, level, levels)
        out_ref[rows * count :] = levels.astype(jnp.int32).astype(jnp.int16)


def coded(x, which):
    _, rows, count, width = x.shape
    vmem = pl.BlockSpec(memory_space=pltpu.VMEM)
    shape = jax.ShapeDtypeStruct((rows * count + 16, width), jnp.int16)
    return pl.pallas_call(
        code_kernel,
        out_shape=[shape] * len(which),
        in_specs=[pl.BlockSpec(memory_space=pltpu.SMEM), vmem],
        out_specs=[vmem] * len(which),
        compiler_params=pltpu.CompilerParams(vmem_limit_bytes=5 * 2**20),
    )(jnp.stack(which), x)


def scales(levels):
    levels = levels.astype(jnp.int32).astype(jnp.float32)
    return jnp.exp2(levels * (1.0 / LEVELS)) * (1.0 / STEPS_MAX)


def decoded_row(ref, scale, r, count):
    q = ref[pl.ds(r * count, count)].astype(jnp.int32).astype(jnp.float32)
    return q * scale[pl.ds(r, 1)]


def finish_kernel(keep_last, which_ref, own_ref, *refs):
    *part_refs, out_ref, edge_ref, scale = refs
    rows, count, _ = out_ref.shape
    for s, ref in enumerate(part_refs):
        scale[s] = scales(ref[rows * count :])
    for r in range(rows):
        x = own_ref[which_ref[0], r]
        for s, ref in enumerate(part_refs):
            x = x + decoded_row(ref, scale.at[s], r, count)
        out_ref[r] = x
        e = r - (rows - HALO) if keep_last else r
        if 0 <= e < HALO:
            edge_ref[e] = x


def finished(own, which, parts, keep_last):
    _, rows, count, width = own.shape
    vmem = pl.BlockSpec(memory_space=pltpu.VMEM)
    shapes = [(rows, count, width), (HALO, count, width)]
    return pl.pallas_call(
        functools.partial(finish_kernel, keep_last),
        out_shape=[jax.ShapeDtypeStruct(x, jnp.float32) for x in shapes],
        in_specs=[pl.BlockSpec(memory_space=pltpu.SMEM)] + [vmem] * (1 + len(parts)),
        out_specs=[vmem] * 2,
        scratch_shapes=[pltpu.VMEM((len(parts), 16, width), jnp.float32)],
        compiler_params=pltpu.CompilerParams(vmem_limit_bytes=6 * 2**20),
    )(jnp.reshape(which, (1,)), own, *parts)


def clear_sides(ref):
    for r in range(ref.shape[0]):
        ref[r, :LEAD] = jnp.zeros((LEAD, ref.shape[2]), jnp.float32)
        ref[r, SPAN - LEAD :] = jnp.zeros((LEAD, ref.shape[2]), jnp.float32)


def mix_kernel(
    which_ref, inv_ref, early_ref, late_ref, own_ref, a_ref, b_ref, c_ref, top_ref, bottom_ref,
    weight_ref,
    mixed_ref, low_ref, high_ref, scale,
):
    half, count, width = early_ref.shape
    quarter = half // 2
    deep = mixed_ref.shape[0]
    inv = inv_ref[...]
    parts = (a_ref, b_ref, c_ref)
    for s, ref in enumerate(parts):
        scale[s] = scales(ref[quarter * count :])
    clear_sides(mixed_ref)
    low_ref[deep] = weight_ref[:8]
    high_ref[deep] = weight_ref[width - 8 :]

    def third(r):
        x = own_ref[which_ref[0], r]
        for s, ref in enumerate(parts):
            x = x + decoded_row(ref, scale.at[s], r, count)
        return x

    def mix_pairs(pairs, slot):
        cat = jnp.concatenate([parts3(x, 0) for pair in pairs for x in pair], axis=1)
        m = jnp.dot(inv, cat, preferred_element_type=jnp.float32)
        for k in range(len(pairs)):
            a = m[:, 2 * k * width : (2 * k + 1) * width]
            b = m[:, (2 * k + 1) * width : (2 * k + 2) * width]
            turned = jnp.transpose(jnp.concatenate([a, b], 0))
            mixed_ref[slot + k, LEAD : LEAD + width] = turned
            low_ref[slot + k] = turned[:8]
            high_ref[slot + k] = turned[width - 8 :]

    mix_pairs([(top_ref[k], early_ref[half - HALO + k]) for k in range(HALO)], 0)
    mix_pairs([(third(k), bottom_ref[k]) for k in range(HALO)], deep - HALO)

    @pl.loop(0, quarter // 2)
    def _(g):
        r = g * 2
        mix_pairs([(early_ref[r + k], third(r + k)) for k in range(2)], r + HALO)
        mix_pairs(
            [(early_ref[r + k + quarter], late_ref[r + k]) for k in range(2)], r + HALO + quarter
        )


def mix(which, inv3, early, late, own, parts, top, bottom, weights):
    half, count, width = early.shape
    deep = half + 2 * HALO
    vmem = pl.BlockSpec(memory_space=pltpu.VMEM)
    shapes = [(deep, SPAN, 2 * count), (deep + 1, 8, 2 * count), (deep + 1, 8, 2 * count)]
    return pl.pallas_call(
        mix_kernel,
        out_shape=[jax.ShapeDtypeStruct(x, jnp.float32) for x in shapes],
        in_specs=[pl.BlockSpec(memory_space=pltpu.SMEM)] + [vmem] * 10,
        out_specs=[vmem] * 3,
        scratch_shapes=[pltpu.VMEM((3, 16, width), jnp.float32)],
        compiler_params=pltpu.CompilerParams(vmem_limit_bytes=10 * 2**20),
    )(jnp.reshape(which, (1,)), inv3, early, late, own, *parts, top, bottom, weights)


def diffuse(src, wh_ref, wv_ref, rows, columns, group, store):
    @pl.loop(0, (columns[1] - columns[0]) // group)
    def _(g):
        c = pl.multiple_of(columns[0] + g * group, 8)
        at, after, before = pl.ds(c, group), pl.ds(c + 1, group), pl.ds(c - 1, group)
        here = src[rows[0], at]
        above = wv_ref[rows[0] - 1, at] * (here - src[rows[0] - 1, at])
        for i in range(*rows):
            below = src[i + 1, at]
            down = wv_ref[i, at] * (below - here)
            right = wh_ref[i, at] * (src[i, after] - here)
            left = wh_ref[i, before] * (here - src[i, before])
            store(i, c, here + (right - left) + (down - above))
            here, above = below, down


def iterate(mixed, y, z, wh_ref, wv_ref, invt_ref, columns, group, together, store):
    deep, lanes = mixed.shape[0], mixed.shape[2]
    length = columns[1] - columns[0]
    used = pl.ds(columns[0], length)
    invt = invt_ref[...]

    def to(ref):
        def put(i, c, value):
            ref[i, pl.ds(c, group)] = value

        return put

    def step(src, rows, put):
        diffuse(src, wh_ref, wv_ref, rows, columns, group, put)

    step(mixed, (1, deep - 1), to(z))
    step(z, (2, deep - 2), to(y))

    @pl.loop(2, deep - 2, step=together)
    def _(first):
        rows = pl.ds(first, together)
        kept = jnp.maximum(y[rows, used], 0.0).reshape(together * length, lanes)
        before = mixed[rows, used].reshape(together * length, lanes)
        u = parts3(kept - 0.5 * before, 1)
        m = jnp.dot(u, invt, preferred_element_type=jnp.float32)
        z[rows, used] = (m + (2.0 * before - kept)).reshape(together, length, lanes)

    step(z, (3, deep - 3), to(y))
    step(y, (4, deep - 4), store)


def inside_kernel(invt_ref, mixed_ref, wh_ref, wv_ref, out_ref, y, z):
    _, width, _ = out_ref.shape
    clear_sides(y)
    clear_sides(z)

    def store(i, c, value):
        out_ref[i - HALO, pl.ds(pl.multiple_of(c - LEAD, 8), GROUP)] = value

    columns = (LEAD, LEAD + width)
    iterate(mixed_ref, y, z, wh_ref, wv_ref, invt_ref, columns, GROUP, 4, store)


def inside(inv3t, mixed, wh, wv, width):
    deep, span, lanes = mixed.shape
    vmem = pl.BlockSpec(memory_space=pltpu.VMEM)
    field = pltpu.VMEM((deep, span, lanes), jnp.float32)
    return pl.pallas_call(
        inside_kernel,
        out_shape=jax.ShapeDtypeStruct((deep - 2 * HALO, width, lanes), jnp.float32),
        in_specs=[vmem] * 4,
        out_specs=vmem,
        scratch_shapes=[field, field],
        compiler_params=pltpu.CompilerParams(vmem_limit_bytes=22 * 2**20),
        cost_estimate=pl.CostEstimate(
            flops=3 * 10**9, bytes_accessed=24 * 2**20, transcendentals=0
        ),
    )(inv3t, mixed, wh, wv)


def sides_kernel(
    invt_ref, left_ref, low_ref, high_ref, right_ref, inside_ref,
    out_ref, mixed, y, z, wh, wv, turned,
):
    half, width, lanes = inside_ref.shape
    count = lanes // 2
    deep, span, _ = mixed.shape
    for ref in (mixed, y, z, wh, wv):
        ref[...] = jnp.zeros(ref.shape, jnp.float32)
    lower = lax.broadcasted_iota(jnp.int32, (8, lanes), 1) < count
    for at, ref in zip((8, 16, 32, 40), (left_ref, low_ref, high_ref, right_ref)):
        mixed[:, at : at + 8] = ref[:deep]
        packed = ref[deep]
        for r in range(deep):
            for weight, lane in ((wh, r), (wv, r + count)):
                one = jnp.broadcast_to(packed[:, lane : lane + 1], (8, lanes))
                two = jnp.broadcast_to(packed[:, lane + half : lane + half + 1], (8, lanes))
                weight[r, at : at + 8] = jnp.where(lower, one, two)

    def store(i, c, value):
        z[i, pl.ds(c, span - 16)] = value

    iterate(
        mixed, y, z, wh, wv, invt_ref, (8, span - 8), span - 16, deep - 4, store
    )
    place = lax.broadcasted_iota(jnp.int32, (8, lanes), 0)

    @pl.loop(0, half // 2)
    def _(g):
        for k in range(2):
            r = g * 2 + k
            first = jnp.where(place < HALO, z[r + HALO, 16:24], inside_ref[r, :8])
            last = jnp.where(place < 8 - HALO, inside_ref[r, width - 8 :], z[r + HALO, 32:40])
            whole = jnp.concatenate([first, inside_ref[r, 8 : width - 8], last], axis=0)
            v = jnp.transpose(jnp.maximum(whole, 0.0))
            for h in range(2):
                for t in range(width // 128):
                    turned[t, pl.ds(r + h * half, count, stride=2 * half), :] = v[
                        h * count : (h + 1) * count, t * 128 : (t + 1) * 128
                    ]

    @pl.loop(0, count // 8)
    def _(g):
        for k in range(8):
            e = g * 8 + k
            for t in range(width // 128):
                out_ref[e, :, t * 128 : (t + 1) * 128] = turned[t, pl.ds(e * 2 * half, 2 * half), :]


def sides(inv3t, left, low, high, right, middle):
    half, width, lanes = middle.shape
    vmem = pl.BlockSpec(memory_space=pltpu.VMEM)
    field = pltpu.VMEM((half + 2 * HALO, 56, lanes), jnp.float32)
    return pl.pallas_call(
        sides_kernel,
        out_shape=jax.ShapeDtypeStruct((lanes // 2, 2 * half, width), jnp.float32),
        in_specs=[vmem] * 6,
        out_specs=vmem,
        scratch_shapes=[
            field,
            field,
            field,
            field,
            field,
            pltpu.VMEM((width // 128, lanes * half, 128), jnp.float32),
        ],
        compiler_params=pltpu.CompilerParams(vmem_limit_bytes=14 * 2**20),
    )(inv3t, left, low, high, right, middle)


def neighbours(axis, low_part, high_part):
    count = lax.axis_size(axis)
    forward = [(i, i + 1) for i in range(count - 1)]
    backward = [(i + 1, i) for i in range(count - 1)]
    return lax.ppermute(high_part, axis, forward), lax.ppermute(low_part, axis, backward)


def raw_weights(weight_h, weight_v):
    col_count = lax.axis_size("col")
    row_count = lax.axis_size("row")
    tile_h, tile_w = weight_h.shape
    rows = lax.axis_index("row") * tile_h + lax.broadcasted_iota(jnp.int32, (tile_h, tile_w), 0)
    cols = lax.axis_index("col") * tile_w + lax.broadcasted_iota(jnp.int32, (tile_h, tile_w), 1)
    wh = jnp.where(cols < tile_w * col_count - 1, weight_h, 0)
    wv = jnp.where(rows < tile_h * row_count - 1, weight_v, 0)
    return jnp.stack([wh, wv]).astype(jnp.bfloat16)


def heightened(weights):
    tile_h = weights.shape[1]
    above, below = neighbours("row", weights[:, :HALO], weights[:, tile_h - HALO :])
    return jnp.concatenate([above, weights, below], axis=1)


def inside_weights(weights):
    tile_w = weights.shape[2]
    return jnp.pad(weights, ((0, 0), (0, 0), (LEAD, SPAN - LEAD - tile_w)))


def packed_weights(weights, count):
    rows, width = weights.shape[1:]
    packed = jnp.pad(weights.astype(jnp.float32), ((0, 0), (0, count - rows), (0, 0)))
    return jnp.transpose(packed.reshape(2 * count, width)) * jnp.float32(KAPPA * EDGE_SCALE)


def last_rows_kernel(which_ref, src_ref, out_ref):
    del which_ref
    out_ref[...] = src_ref[...].reshape(out_ref.shape)


def last_rows(source, which, rows):
    blocks, _, bands, height, width = source.shape
    at = height // rows - 1
    return pl.pallas_call(
        last_rows_kernel,
        grid_spec=pltpu.PrefetchScalarGridSpec(
            num_scalar_prefetch=1,
            grid=(blocks,),
            in_specs=[
                pl.BlockSpec((1, 1, bands, rows, width), lambda s, which: (s, which[0], 0, at, 0))
            ],
            out_specs=pl.BlockSpec((1, bands, rows, width), lambda s, which: (s, 0, 0, 0)),
        ),
        out_shape=jax.ShapeDtypeStruct((blocks, bands, rows, width), source.dtype),
    )(jnp.reshape(which, (1,)), source)


def held_weights(weights, count, half):
    deep = half + 2 * HALO
    pair = jnp.stack([weights[:, :deep], weights[:, half:]]).astype(jnp.bfloat16)
    lanes = lax.broadcasted_iota(jnp.int32, (2, 2 * count), 1) // count
    spread = (lanes == lax.broadcasted_iota(jnp.int32, (2, 2 * count), 0)).astype(jnp.bfloat16)
    scale = jnp.float32(KAPPA * EDGE_SCALE)
    return [
        scale * jnp.einsum("hrc,hl->rcl", x, spread, preferred_element_type=jnp.float32)
        for x in (pair[:, 0], pair[:, 1])
    ]


def per_device(cube, library_t, inverse, weight_h, weight_v):
    strips, bands, tile_h, tile_w = cube.shape
    count = library_t.shape[0]
    half, quarter = tile_h // 2, tile_h // 4
    ys = strips // 2
    col = lax.axis_index("col").astype(jnp.int32)
    y, x = lax.shift_right_logical(col, 1), lax.bitwise_and(col, 1)
    columns = [[c for c in range(strips) if c % 2 == k] for k in range(2)]
    swap = [(c, c ^ 1) for c in range(strips)]
    turns = [[(c, (c + 2 * k) % strips) for c in range(strips)] for k in range(ys)]
    barrier = lax.optimization_barrier

    def project(library, block, blocks, rows):
        block = block.reshape(-1, blocks * rows, tile_w)
        p = jnp.einsum("eb,bhw->hew", library, block, preferred_element_type=jnp.float32)
        return p.reshape(blocks, rows, count, tile_w)

    def rows_of(source, side, begin):
        rows = source[:, :, :, begin : begin + quarter]
        rows = jnp.where(side == 0, rows[:, 0], rows[:, 1])
        return jnp.transpose(rows, (1, 0, 2, 3)).reshape(bands, half * 2, tile_w)

    library_own = lax.dynamic_slice_in_dim(library_t, col * bands, bands, axis=1)
    library_pair = lax.dynamic_slice_in_dim(library_t, (col ^ 1) * bands, bands, axis=1)
    library_x = jnp.concatenate([library_own, library_pair], axis=1)
    split = [library_t[:, k * bands : (k + 1) * bands] for k in range(strips)]
    library_y = jnp.where(
        x == 0, jnp.concatenate(split[::2], axis=1), jnp.concatenate(split[1::2], axis=1)
    )

    by_y = cube.reshape(ys, 2, bands, tile_h, tile_w)
    early = jnp.transpose(by_y[..., :half, :], (0, 2, 1, 3, 4))
    early = early.reshape(ys, bands, 2 * half, tile_w)
    early, by_y = barrier((early, by_y))
    late = rows_of(by_y, 1 - x, 3 * quarter)
    late, by_y = barrier((late, by_y))
    third = rows_of(by_y, 1 - x, half)
    early = lax.all_to_all(
        early, "col", split_axis=0, concat_axis=0, axis_index_groups=columns, tiled=True
    )
    late = lax.ppermute(late, "col", swap)
    third, by_y = barrier((third, by_y))
    own, weight_h, weight_v, _ = barrier((last_rows(by_y, x, half), weight_h, weight_v, third))
    weights = heightened(raw_weights(weight_h, weight_v))
    wh, wv = held_weights(inside_weights(weights), count, half)

    def own_rows(begin):
        rows = jnp.transpose(own[:, :, begin : begin + quarter], (1, 0, 2, 3))
        return rows.reshape(bands, ys * quarter, tile_w)

    third_own, late_own = own_rows(0), own_rows(quarter)
    order = [lax.bitwise_and(y + k, ys - 1) for k in range(1, ys)]

    def over_y(parts):
        return [lax.ppermute(p, "col", turns[k + 1]) for k, p in enumerate(parts)]

    third, late = barrier((third, late))
    third = lax.ppermute(third, "col", swap)
    late = project(library_x, jnp.concatenate([late_own, late], axis=0), ys, quarter)
    late_coded = coded(late, order)
    wh, wv, late_coded = barrier((wh, wv, late_coded))
    late_coded = over_y(late_coded)
    early = project(library_y, early, 2, half)
    early_coded = coded(early, [1 - x])[0]
    third, late_coded, _ = barrier((third, late_coded, early_coded))
    early_coded = lax.ppermute(early_coded, "col", swap)
    third = project(library_x, jnp.concatenate([third_own, third], axis=0), ys, quarter)
    third_coded = coded(third, order)
    late_coded, _ = barrier((late_coded, third_coded))
    packed = packed_weights(weights, count)
    third_coded = over_y(third_coded)
    late, last = finished(late, y, late_coded, True)
    early, first = finished(early, x, [early_coded], False)
    top, bottom = neighbours("row", first, last)

    inv_hi = lax.reduce_precision(inverse, 8, 7)
    inv3 = jnp.concatenate([inv_hi, inverse - inv_hi, inv_hi], axis=1).astype(jnp.bfloat16)
    block = lax.broadcasted_iota(jnp.int32, (2 * count, 2 * count), 0) // count
    block = block == lax.broadcasted_iota(jnp.int32, (2 * count, 2 * count), 1) // count
    twice = jnp.where(block, jnp.tile(inverse.T, (2, 2)), 0.0)
    twice_hi = lax.reduce_precision(twice, 8, 7)
    inv3t = jnp.concatenate([twice_hi, twice - twice_hi, twice_hi], axis=0).astype(jnp.bfloat16)
    mixed, low, high = mix(y, inv3, early, late, third, third_coded, top, bottom, packed)
    left, right = neighbours("col", low, high)
    weights_in, _ = barrier((inside_weights(weights), low))
    wv = held_weights(weights_in, count, half)[1]
    middle = inside(inv3t, mixed, wh, wv, tile_w)
    return sides(inv3t, left, low, high, right, middle)


def solution(mesh):
    return jax.shard_map(
        per_device,
        mesh=mesh,
        in_specs=(P(None, "col", "row", None), P(), P(), P("row", "col"), P("row", "col")),
        out_specs=P(None, "row", "col"),
        check_vma=False,
    )
```

```python
import functools

import jax
import jax.numpy as jnp
from jax import lax
from jax.experimental import pallas as pl
from jax.experimental.pallas import tpu as pltpu
from jax.sharding import PartitionSpec as P

KAPPA = 0.24
EDGE_SCALE = 1.0 / 255.0
HALO = 4
LEAD = 16
SPAN = 288
GROUP = 128
LEVELS = 256.0
STEPS_MAX = 32000.0


def parts3(x, axis):
    hi = x.astype(jnp.bfloat16)
    lo = (x - hi.astype(jnp.float32)).astype(jnp.bfloat16)
    return jnp.concatenate([hi, hi, lo], axis=axis)


def code_kernel(which_ref, x_ref, *out_refs):
    _, rows, count, width = x_ref.shape
    slot = lax.broadcasted_iota(jnp.int32, (16, width), 0)
    for s, out_ref in enumerate(out_refs):
        levels = jnp.zeros((16, width), jnp.float32)
        for r in range(rows):
            x = x_ref[which_ref[s], r]
            top = jnp.max(jnp.max(jnp.abs(x), axis=0, keepdims=True), axis=1, keepdims=True)
            level = jnp.ceil(jnp.log2(jnp.maximum(top, 1e-30)) * LEVELS)
            scale = STEPS_MAX * jnp.exp2(level * (-1.0 / LEVELS))
            q = jnp.round(x * scale).astype(jnp.int32).astype(jnp.int16)
            out_ref[r * count : (r + 1) * count] = q
            levels = jnp.where(slot == r, level, levels)
        out_ref[rows * count :] = levels.astype(jnp.int32).astype(jnp.int16)


def coded(x, which):
    _, rows, count, width = x.shape
    vmem = pl.BlockSpec(memory_space=pltpu.VMEM)
    shape = jax.ShapeDtypeStruct((rows * count + 16, width), jnp.int16)
    return pl.pallas_call(
        code_kernel,
        out_shape=[shape] * len(which),
        in_specs=[pl.BlockSpec(memory_space=pltpu.SMEM), vmem],
        out_specs=[vmem] * len(which),
        compiler_params=pltpu.CompilerParams(vmem_limit_bytes=5 * 2**20),
    )(jnp.stack(which), x)


def scales(levels):
    levels = levels.astype(jnp.int32).astype(jnp.float32)
    return jnp.exp2(levels * (1.0 / LEVELS)) * (1.0 / STEPS_MAX)


def decoded_row(ref, scale, r, count):
    q = ref[pl.ds(r * count, count)].astype(jnp.int32).astype(jnp.float32)
    return q * scale[pl.ds(r, 1)]


def finish_kernel(keep_last, which_ref, own_ref, *refs):
    *part_refs, out_ref, edge_ref, scale = refs
    rows, count, _ = out_ref.shape
    for s, ref in enumerate(part_refs):
        scale[s] = scales(ref[rows * count :])
    for r in range(rows):
        x = own_ref[which_ref[0], r]
        for s, ref in enumerate(part_refs):
            x = x + decoded_row(ref, scale.at[s], r, count)
        out_ref[r] = x
        e = r - (rows - HALO) if keep_last else r
        if 0 <= e < HALO:
            edge_ref[e] = x


def finished(own, which, parts, keep_last):
    _, rows, count, width = own.shape
    vmem = pl.BlockSpec(memory_space=pltpu.VMEM)
    shapes = [(rows, count, width), (HALO, count, width)]
    return pl.pallas_call(
        functools.partial(finish_kernel, keep_last),
        out_shape=[jax.ShapeDtypeStruct(x, jnp.float32) for x in shapes],
        in_specs=[pl.BlockSpec(memory_space=pltpu.SMEM)] + [vmem] * (1 + len(parts)),
        out_specs=[vmem] * 2,
        scratch_shapes=[pltpu.VMEM((len(parts), 16, width), jnp.float32)],
        compiler_params=pltpu.CompilerParams(vmem_limit_bytes=6 * 2**20),
    )(jnp.reshape(which, (1,)), own, *parts)


def clear_sides(ref):
    for r in range(ref.shape[0]):
        ref[r, :LEAD] = jnp.zeros((LEAD, ref.shape[2]), jnp.float32)
        ref[r, SPAN - LEAD :] = jnp.zeros((LEAD, ref.shape[2]), jnp.float32)


def mix_kernel(
    which_ref, inv_ref, early_ref, late_ref, own_ref, a_ref, b_ref, c_ref, top_ref, bottom_ref,
    weight_ref,
    mixed_ref, low_ref, high_ref, scale,
):
    half, count, width = early_ref.shape
    quarter = half // 2
    deep = mixed_ref.shape[0]
    inv = inv_ref[...]
    parts = (a_ref, b_ref, c_ref)
    for s, ref in enumerate(parts):
        scale[s] = scales(ref[quarter * count :])
    clear_sides(mixed_ref)
    low_ref[deep] = weight_ref[:8]
    high_ref[deep] = weight_ref[width - 8 :]

    def third(r):
        x = own_ref[which_ref[0], r]
        for s, ref in enumerate(parts):
            x = x + decoded_row(ref, scale.at[s], r, count)
        return x

    def mix_pairs(pairs, slot):
        cat = jnp.concatenate([parts3(x, 0) for pair in pairs for x in pair], axis=1)
        m = jnp.dot(inv, cat, preferred_element_type=jnp.float32)
        for k in range(len(pairs)):
            a = m[:, 2 * k * width : (2 * k + 1) * width]
            b = m[:, (2 * k + 1) * width : (2 * k + 2) * width]
            turned = jnp.transpose(jnp.concatenate([a, b], 0))
            mixed_ref[slot + k, LEAD : LEAD + width] = turned
            low_ref[slot + k] = turned[:8]
            high_ref[slot + k] = turned[width - 8 :]

    mix_pairs([(top_ref[k], early_ref[half - HALO + k]) for k in range(HALO)], 0)
    mix_pairs([(third(k), bottom_ref[k]) for k in range(HALO)], deep - HALO)

    @pl.loop(0, quarter // 2)
    def _(g):
        r = g * 2
        mix_pairs([(early_ref[r + k], third(r + k)) for k in range(2)], r + HALO)
        mix_pairs(
            [(early_ref[r + k + quarter], late_ref[r + k]) for k in range(2)], r + HALO + quarter
        )


def mix(which, inv3, early, late, own, parts, top, bottom, weights):
    half, count, width = early.shape
    deep = half + 2 * HALO
    vmem = pl.BlockSpec(memory_space=pltpu.VMEM)
    shapes = [(deep, SPAN, 2 * count), (deep + 1, 8, 2 * count), (deep + 1, 8, 2 * count)]
    return pl.pallas_call(
        mix_kernel,
        out_shape=[jax.ShapeDtypeStruct(x, jnp.float32) for x in shapes],
        in_specs=[pl.BlockSpec(memory_space=pltpu.SMEM)] + [vmem] * 10,
        out_specs=[vmem] * 3,
        scratch_shapes=[pltpu.VMEM((3, 16, width), jnp.float32)],
        compiler_params=pltpu.CompilerParams(vmem_limit_bytes=10 * 2**20),
    )(jnp.reshape(which, (1,)), inv3, early, late, own, *parts, top, bottom, weights)


def diffuse(src, wh_ref, wv_ref, rows, columns, group, store):
    @pl.loop(0, (columns[1] - columns[0]) // group)
    def _(g):
        c = pl.multiple_of(columns[0] + g * group, 8)
        at, after, before = pl.ds(c, group), pl.ds(c + 1, group), pl.ds(c - 1, group)
        here = src[rows[0], at]
        above = wv_ref[rows[0] - 1, at] * (here - src[rows[0] - 1, at])
        for i in range(*rows):
            below = src[i + 1, at]
            down = wv_ref[i, at] * (below - here)
            right = wh_ref[i, at] * (src[i, after] - here)
            left = wh_ref[i, before] * (here - src[i, before])
            store(i, c, here + (right - left) + (down - above))
            here, above = below, down


def iterate(mixed, y, z, wh_ref, wv_ref, invt_ref, columns, group, together, store):
    deep, lanes = mixed.shape[0], mixed.shape[2]
    length = columns[1] - columns[0]
    used = pl.ds(columns[0], length)
    invt = invt_ref[...]

    def to(ref):
        def put(i, c, value):
            ref[i, pl.ds(c, group)] = value

        return put

    def step(src, rows, put):
        diffuse(src, wh_ref, wv_ref, rows, columns, group, put)

    step(mixed, (1, deep - 1), to(z))
    step(z, (2, deep - 2), to(y))

    @pl.loop(2, deep - 2, step=together)
    def _(first):
        rows = pl.ds(first, together)
        kept = jnp.maximum(y[rows, used], 0.0).reshape(together * length, lanes)
        before = mixed[rows, used].reshape(together * length, lanes)
        u = parts3(kept - 0.5 * before, 1)
        m = jnp.dot(u, invt, preferred_element_type=jnp.float32)
        z[rows, used] = (m + (2.0 * before - kept)).reshape(together, length, lanes)

    step(z, (3, deep - 3), to(y))
    step(y, (4, deep - 4), store)


def inside_kernel(invt_ref, mixed_ref, wh_ref, wv_ref, out_ref, y, z):
    _, width, _ = out_ref.shape
    clear_sides(y)
    clear_sides(z)

    def store(i, c, value):
        out_ref[i - HALO, pl.ds(pl.multiple_of(c - LEAD, 8), GROUP)] = value

    columns = (LEAD, LEAD + width)
    iterate(mixed_ref, y, z, wh_ref, wv_ref, invt_ref, columns, GROUP, 4, store)


def inside(inv3t, mixed, wh, wv, width):
    deep, span, lanes = mixed.shape
    vmem = pl.BlockSpec(memory_space=pltpu.VMEM)
    field = pltpu.VMEM((deep, span, lanes), jnp.float32)
    return pl.pallas_call(
        inside_kernel,
        out_shape=jax.ShapeDtypeStruct((deep - 2 * HALO, width, lanes), jnp.float32),
        in_specs=[vmem] * 4,
        out_specs=vmem,
        scratch_shapes=[field, field],
        compiler_params=pltpu.CompilerParams(vmem_limit_bytes=22 * 2**20),
        cost_estimate=pl.CostEstimate(
            flops=3 * 10**9, bytes_accessed=24 * 2**20, transcendentals=0
        ),
    )(inv3t, mixed, wh, wv)


def sides_kernel(
    invt_ref, left_ref, low_ref, high_ref, right_ref, inside_ref,
    out_ref, mixed, y, z, wh, wv, turned,
):
    half, width, lanes = inside_ref.shape
    count = lanes // 2
    deep, span, _ = mixed.shape
    for ref in (mixed, y, z, wh, wv):
        ref[...] = jnp.zeros(ref.shape, jnp.float32)
    lower = lax.broadcasted_iota(jnp.int32, (8, lanes), 1) < count
    for at, ref in zip((8, 16, 32, 40), (left_ref, low_ref, high_ref, right_ref)):
        mixed[:, at : at + 8] = ref[:deep]
        packed = ref[deep]
        for r in range(deep):
            for weight, lane in ((wh, r), (wv, r + count)):
                one = jnp.broadcast_to(packed[:, lane : lane + 1], (8, lanes))
                two = jnp.broadcast_to(packed[:, lane + half : lane + half + 1], (8, lanes))
                weight[r, at : at + 8] = jnp.where(lower, one, two)

    def store(i, c, value):
        z[i, pl.ds(c, span - 16)] = value

    iterate(
        mixed, y, z, wh, wv, invt_ref, (8, span - 8), span - 16, deep - 4, store
    )
    place = lax.broadcasted_iota(jnp.int32, (8, lanes), 0)

    @pl.loop(0, half // 4)
    def _(g):
        for k in range(4):
            r = g * 4 + k
            first = jnp.where(place < HALO, z[r + HALO, 16:24], inside_ref[r, :8])
            last = jnp.where(place < 8 - HALO, inside_ref[r, width - 8 :], z[r + HALO, 32:40])
            whole = jnp.concatenate([first, inside_ref[r, 8 : width - 8], last], axis=0)
            v = jnp.transpose(jnp.maximum(whole, 0.0))
            for h in range(2):
                for t in range(width // 128):
                    turned[t, pl.ds(r + h * half, count, stride=2 * half), :] = v[
                        h * count : (h + 1) * count, t * 128 : (t + 1) * 128
                    ]

    @pl.loop(0, count // 8)
    def _(g):
        for k in range(8):
            e = g * 8 + k
            for t in range(width // 128):
                out_ref[e, :, t * 128 : (t + 1) * 128] = turned[t, pl.ds(e * 2 * half, 2 * half), :]


def sides(inv3t, left, low, high, right, middle):
    half, width, lanes = middle.shape
    vmem = pl.BlockSpec(memory_space=pltpu.VMEM)
    field = pltpu.VMEM((half + 2 * HALO, 56, lanes), jnp.float32)
    return pl.pallas_call(
        sides_kernel,
        out_shape=jax.ShapeDtypeStruct((lanes // 2, 2 * half, width), jnp.float32),
        in_specs=[vmem] * 6,
        out_specs=vmem,
        scratch_shapes=[
            field,
            field,
            field,
            field,
            field,
            pltpu.VMEM((width // 128, lanes * half, 128), jnp.float32),
        ],
        compiler_params=pltpu.CompilerParams(vmem_limit_bytes=14 * 2**20),
    )(inv3t, left, low, high, right, middle)


def neighbours(axis, low_part, high_part):
    count = lax.axis_size(axis)
    forward = [(i, i + 1) for i in range(count - 1)]
    backward = [(i + 1, i) for i in range(count - 1)]
    return lax.ppermute(high_part, axis, forward), lax.ppermute(low_part, axis, backward)


def raw_weights(weight_h, weight_v):
    col_count = lax.axis_size("col")
    row_count = lax.axis_size("row")
    tile_h, tile_w = weight_h.shape
    rows = lax.axis_index("row") * tile_h + lax.broadcasted_iota(jnp.int32, (tile_h, tile_w), 0)
    cols = lax.axis_index("col") * tile_w + lax.broadcasted_iota(jnp.int32, (tile_h, tile_w), 1)
    wh = jnp.where(cols < tile_w * col_count - 1, weight_h, 0)
    wv = jnp.where(rows < tile_h * row_count - 1, weight_v, 0)
    return jnp.stack([wh, wv]).astype(jnp.bfloat16)


def heightened(weights):
    tile_h = weights.shape[1]
    above, below = neighbours("row", weights[:, :HALO], weights[:, tile_h - HALO :])
    return jnp.concatenate([above, weights, below], axis=1)


def inside_weights(weights):
    tile_w = weights.shape[2]
    return jnp.pad(weights, ((0, 0), (0, 0), (LEAD, SPAN - LEAD - tile_w)))


def packed_weights(weights, count):
    rows, width = weights.shape[1:]
    packed = jnp.pad(weights.astype(jnp.float32), ((0, 0), (0, count - rows), (0, 0)))
    return jnp.transpose(packed.reshape(2 * count, width)) * jnp.float32(KAPPA * EDGE_SCALE)


def last_rows_kernel(which_ref, src_ref, out_ref):
    del which_ref
    out_ref[...] = src_ref[...].reshape(out_ref.shape)


def last_rows(source, which, rows):
    blocks, _, bands, height, width = source.shape
    at = height // rows - 1
    return pl.pallas_call(
        last_rows_kernel,
        grid_spec=pltpu.PrefetchScalarGridSpec(
            num_scalar_prefetch=1,
            grid=(blocks,),
            in_specs=[
                pl.BlockSpec((1, 1, bands, rows, width), lambda s, which: (s, which[0], 0, at, 0))
            ],
            out_specs=pl.BlockSpec((1, bands, rows, width), lambda s, which: (s, 0, 0, 0)),
        ),
        out_shape=jax.ShapeDtypeStruct((blocks, bands, rows, width), source.dtype),
    )(jnp.reshape(which, (1,)), source)


def held_weights(weights, count, half):
    deep = half + 2 * HALO
    pair = jnp.stack([weights[:, :deep], weights[:, half:]]).astype(jnp.bfloat16)
    lanes = lax.broadcasted_iota(jnp.int32, (2, 2 * count), 1) // count
    spread = (lanes == lax.broadcasted_iota(jnp.int32, (2, 2 * count), 0)).astype(jnp.bfloat16)
    scale = jnp.float32(KAPPA * EDGE_SCALE)
    return [
        scale * jnp.einsum("hrc,hl->rcl", x, spread, preferred_element_type=jnp.float32)
        for x in (pair[:, 0], pair[:, 1])
    ]


def per_device(cube, library_t, inverse, weight_h, weight_v):
    strips, bands, tile_h, tile_w = cube.shape
    count = library_t.shape[0]
    half, quarter = tile_h // 2, tile_h // 4
    ys = strips // 2
    col = lax.axis_index("col").astype(jnp.int32)
    y, x = lax.shift_right_logical(col, 1), lax.bitwise_and(col, 1)
    columns = [[c for c in range(strips) if c % 2 == k] for k in range(2)]
    swap = [(c, c ^ 1) for c in range(strips)]
    turns = [[(c, (c + 2 * k) % strips) for c in range(strips)] for k in range(ys)]
    barrier = lax.optimization_barrier

    def project(library, block, blocks, rows):
        block = block.reshape(-1, blocks * rows, tile_w)
        p = jnp.einsum("eb,bhw->hew", library, block, preferred_element_type=jnp.float32)
        return p.reshape(blocks, rows, count, tile_w)

    def rows_of(source, side, begin):
        rows = source[:, :, :, begin : begin + quarter]
        rows = jnp.where(side == 0, rows[:, 0], rows[:, 1])
        return jnp.transpose(rows, (1, 0, 2, 3)).reshape(bands, half * 2, tile_w)

    library_own = lax.dynamic_slice_in_dim(library_t, col * bands, bands, axis=1)
    library_pair = lax.dynamic_slice_in_dim(library_t, (col ^ 1) * bands, bands, axis=1)
    library_x = jnp.concatenate([library_own, library_pair], axis=1)
    split = [library_t[:, k * bands : (k + 1) * bands] for k in range(strips)]
    library_y = jnp.where(
        x == 0, jnp.concatenate(split[::2], axis=1), jnp.concatenate(split[1::2], axis=1)
    )

    by_y = cube.reshape(ys, 2, bands, tile_h, tile_w)
    early = jnp.transpose(by_y[..., :half, :], (0, 2, 1, 3, 4))
    early = early.reshape(ys, bands, 2 * half, tile_w)
    early, by_y = barrier((early, by_y))
    late = rows_of(by_y, 1 - x, 3 * quarter)
    late, by_y = barrier((late, by_y))
    third = rows_of(by_y, 1 - x, half)
    early = lax.all_to_all(
        early, "col", split_axis=0, concat_axis=0, axis_index_groups=columns, tiled=True
    )
    late = lax.ppermute(late, "col", swap)
    third, by_y = barrier((third, by_y))
    own, weight_h, weight_v, _ = barrier((last_rows(by_y, x, half), weight_h, weight_v, third))
    weights = heightened(raw_weights(weight_h, weight_v))
    wh, wv = held_weights(inside_weights(weights), count, half)

    def own_rows(begin):
        rows = jnp.transpose(own[:, :, begin : begin + quarter], (1, 0, 2, 3))
        return rows.reshape(bands, ys * quarter, tile_w)

    third_own, late_own = own_rows(0), own_rows(quarter)
    order = [lax.bitwise_and(y + k, ys - 1) for k in range(1, ys)]

    def over_y(parts):
        return [lax.ppermute(p, "col", turns[k + 1]) for k, p in enumerate(parts)]

    third, late = barrier((third, late))
    third = lax.ppermute(third, "col", swap)
    late = project(library_x, jnp.concatenate([late_own, late], axis=0), ys, quarter)
    late_coded = coded(late, order)
    wh, wv, late_coded = barrier((wh, wv, late_coded))
    late_coded = over_y(late_coded)
    early = project(library_y, early, 2, half)
    early_coded = coded(early, [1 - x])[0]
    third, late_coded, _ = barrier((third, late_coded, early_coded))
    early_coded = lax.ppermute(early_coded, "col", swap)
    third = project(library_x, jnp.concatenate([third_own, third], axis=0), ys, quarter)
    third_coded = coded(third, order)
    late_coded, _ = barrier((late_coded, third_coded))
    packed = packed_weights(weights, count)
    third_coded = over_y(third_coded)
    late, last = finished(late, y, late_coded, True)
    early, first = finished(early, x, [early_coded], False)
    top, bottom = neighbours("row", first, last)

    inv_hi = lax.reduce_precision(inverse, 8, 7)
    inv3 = jnp.concatenate([inv_hi, inverse - inv_hi, inv_hi], axis=1).astype(jnp.bfloat16)
    block = lax.broadcasted_iota(jnp.int32, (2 * count, 2 * count), 0) // count
    block = block == lax.broadcasted_iota(jnp.int32, (2 * count, 2 * count), 1) // count
    twice = jnp.where(block, jnp.tile(inverse.T, (2, 2)), 0.0)
    twice_hi = lax.reduce_precision(twice, 8, 7)
    inv3t = jnp.concatenate([twice_hi, twice - twice_hi, twice_hi], axis=0).astype(jnp.bfloat16)
    mixed, low, high = mix(y, inv3, early, late, third, third_coded, top, bottom, packed)
    left, right = neighbours("col", low, high)
    weights_in, _ = barrier((inside_weights(weights), low))
    wv = held_weights(weights_in, count, half)[1]
    middle = inside(inv3t, mixed, wh, wv, tile_w)
    return sides(inv3t, left, low, high, right, middle)


def solution(mesh):
    return jax.shard_map(
        per_device,
        mesh=mesh,
        in_specs=(P(None, "col", "row", None), P(), P(), P("row", "col"), P("row", "col")),
        out_specs=P(None, "row", "col"),
        check_vma=False,
    )
```
